1024 devices in a mesh: leaf: 64 (over y_hi, z, core), grp: 16 (over y_lo, x).
Axes of the slice: x: 4, y: 8 (y_hi: 2, y_lo: 4; y = y_hi * 4 + y_lo), z: 16, core: 2. Of those that a mesh axis runs over, the one named last changes fastest.
Arguments:
- charges: bfloat16 [32768, 16, 128], P(('leaf', 'grp')), may hold values from -6 to 6
- points: bfloat16 [32768, 3, 128], P(('leaf', 'grp')), may hold values from 0 to 13
- near_list: int32 [32768, 20], P(('leaf', 'grp')), may hold values from 0 to 32767, as said below
- near_count: int32 [32768], P(('leaf', 'grp')), may hold values from 1 to 20
- basis: bfloat16 [32768, 64, 128], P(('leaf', 'grp')), may hold values from -0.5 to 0.5
- far_list: int32 [32768, 6], P(('leaf', 'grp')), may hold values from 0 to 32767, as said below
- leaf_coupling_stack: bfloat16 [32768, 64, 384], P(('leaf', 'grp')), may hold values from -0.3125 to 0.3125
- transfer: bfloat16 [1024, 64, 2048], P(('leaf', 'grp')), may hold values from -0.375 to 0.375
- node_list: int32 [1024, 2], P(('leaf', 'grp')), may hold values from 0 to 15, as said below
- node_coupling: bfloat16 [1024, 64, 128], P(('leaf', 'grp')), may hold values from -0.5 to 0.5
- lift: bfloat16 [64, 16, 64, 64], P('leaf'), may hold values from -0.375 to 0.375
- top_list: int32 [64, 4], P('leaf'), may hold values from 0 to 63, as said below
- top_coupling: bfloat16 [64, 64, 256], P('leaf'), may hold values from -0.375 to 0.375
Outputs:
- potentials: bfloat16 [32768, 16, 128], P(('leaf', 'grp'))
The draws below stay inside these ranges and needn't reach their ends.
Inputs may be any that keep to these rules, and one draw needn't show every extreme that they name: `near_list`: row t lists leaf t first, then 20 - 1 distinct other leaves whose cyclic distance to t in tree order is 1 to 12. `far_list`: row t lists 6 distinct leaves whose cyclic distance to t in tree order is 13 to 20. `node_list`: row n lists distinct indices within node n's group, never n mod 16 itself. `top_list`: row g lists distinct groups other than g.
All inputs are finite; a program needn't handle non-finite values.
Results may differ from the reference program's by a relative error of at most 0.015.
Values may be sent and summed in bfloat16 or wider, within the bound.
A program may use at most 32 MiB of HBM per device.

```python
import jax
import jax.numpy as jnp
from jax import lax

LEAVES_PER_UNIT = 32
LEAF_SIZE = 128
COUPLING_RANK = 64
RIGHT_SIDES = 16
NEAR_BLOCKS = 20
NEAR_REACH = 12
FAR_LEAVES = 6
FAR_REACH = 20
NODE_SOURCES = 2
TOP_SOURCES = 4
LEAVES = 32768
NODE_COUNT = 1024
SUBTREES = 16
GROUPS = 64


def select_unique_sources(key, row_total, candidates, chosen_count):
    scores = jax.random.randint(key, (row_total, candidates), 0, 1 << 20) * candidates
    scores = scores + jnp.arange(candidates, dtype=jnp.int32)[None, :]
    unused, chosen = lax.top_k(scores, chosen_count)
    return chosen.astype(jnp.int32)


def draw_near_list(key, part):
    key = jax.random.fold_in(key, 11)
    chosen = select_unique_sources(key, LEAVES, 2 * NEAR_REACH, NEAR_BLOCKS - 1)
    offsets = jnp.where(chosen < NEAR_REACH, chosen - NEAR_REACH, chosen - NEAR_REACH + 1)
    leaf_cluster_index = jnp.arange(LEAVES, dtype=jnp.int32)[:, None]
    others = jnp.mod(leaf_cluster_index + offsets, LEAVES)
    return jnp.concatenate([leaf_cluster_index, others], 1).astype(jnp.int32)


def draw_far_list(key, part):
    key = jax.random.fold_in(key, 23)
    span_size = FAR_REACH - NEAR_REACH
    chosen = select_unique_sources(key, LEAVES, 2 * span_size, FAR_LEAVES)
    offsets = jnp.where(chosen < span_size, -(NEAR_REACH + 1 + chosen), NEAR_REACH + 1 + chosen - span_size)
    leaf_cluster_index = jnp.arange(LEAVES, dtype=jnp.int32)[:, None]
    return jnp.mod(leaf_cluster_index + offsets, LEAVES).astype(jnp.int32)


def draw_node_list(key, part):
    key = jax.random.fold_in(key, 37)
    chosen = select_unique_sources(key, NODE_COUNT, SUBTREES - 1, NODE_SOURCES)
    own_index = jnp.mod(jnp.arange(NODE_COUNT, dtype=jnp.int32), SUBTREES)
    return jnp.mod(own_index[:, None] + 1 + chosen, SUBTREES).astype(jnp.int32)


def draw_top_list(key, part):
    key = jax.random.fold_in(key, 41)
    chosen = select_unique_sources(key, GROUPS, GROUPS - 1, TOP_SOURCES)
    group_ids = jnp.arange(GROUPS, dtype=jnp.int32)
    return jnp.mod(group_ids[:, None] + 1 + chosen, GROUPS).astype(jnp.int32)


def plant(array, stream_key, smallest, largest):
    longest = array.shape.index(max(array.shape))
    spots = []
    for shift in (0, 1):
        where = [jax.random.randint(jax.random.fold_in(stream_key, axis), (), 0, length) for axis, length in enumerate(array.shape)]
        where[longest] = (where[longest] + shift) % array.shape[longest]
        spots.append(tuple(where))
    return array.at[spots[0]].set(smallest).at[spots[1]].set(largest)


def block_levels(rng, dims, split, least, largest):
    def one(dim, parts):
        steps = jax.random.uniform(jax.random.fold_in(jax.random.fold_in(rng, 6), dim), (parts,), jnp.float32, least / len(split), largest / len(split))
        return jnp.repeat(jnp.exp(steps), dims[dim] // parts).reshape((-1,) + (1,) * (len(dims) - dim - 1))

    gain = one(*split[0])
    for cut in split[1:]:
        gain = gain * one(*cut)
    return gain


def normal_values(stream_key, extent, width, bound, shards=(), kind=jnp.bfloat16):
    loudness = block_levels(stream_key, extent, shards, -0.22, 0.18) if shards else 1.0
    array = jax.random.normal(stream_key, extent, jnp.float32) * width * loudness
    return jnp.minimum(jnp.maximum(array, -bound), bound).astype(kind)


def setup_inputs(seed: int = 0) -> dict:
    splits = jax.random.split(jax.random.key(seed), 14)
    return {
        "charges": normal_values(splits[0], (LEAVES, RIGHT_SIDES, LEAF_SIZE), 1.0, 6.0, ((0, 1024),)),
        "points": jnp.clip(13.0 * jax.random.uniform(splits[1], (LEAVES, 3, LEAF_SIZE), jnp.float32) ** block_levels(splits[1], (LEAVES, 3, LEAF_SIZE), ((0, 1024),), -0.2, 0.2), 0.0, 13.0).astype(jnp.bfloat16),
        "near_list": draw_near_list(jax.random.fold_in(splits[13], 71), 0),
        "near_count": plant(jax.random.randint(splits[3], (LEAVES,), 1, NEAR_BLOCKS + 1), jax.random.fold_in(splits[3], 1), 1, NEAR_BLOCKS).astype(jnp.int32),
        "basis": normal_values(splits[4], (LEAVES, COUPLING_RANK, LEAF_SIZE), LEAF_SIZE ** -0.5, 0.5, ((0, 1024),)),
        "far_list": draw_far_list(jax.random.fold_in(splits[13], 71), 0),
        "leaf_coupling_stack": normal_values(splits[6], (LEAVES, COUPLING_RANK, FAR_LEAVES * COUPLING_RANK), (FAR_LEAVES * COUPLING_RANK) ** -0.5, 0.3125, ((0, 1024),)),
        "transfer": normal_values(splits[7], (NODE_COUNT, COUPLING_RANK, LEAVES_PER_UNIT * COUPLING_RANK), (COUPLING_RANK * 4) ** -0.5, 0.375, ((0, 1024),)),
        "node_list": draw_node_list(jax.random.fold_in(splits[13], 71), 0),
        "node_coupling": normal_values(splits[9], (NODE_COUNT, COUPLING_RANK, NODE_SOURCES * COUPLING_RANK), (NODE_SOURCES * COUPLING_RANK) ** -0.5, 0.5, ((0, 1024),)),
        "lift": normal_values(splits[10], (GROUPS, SUBTREES, COUPLING_RANK, COUPLING_RANK), (COUPLING_RANK * 4) ** -0.5, 0.375, ((0, 64),)),
        "top_list": draw_top_list(jax.random.fold_in(splits[13], 71), 0),
        "top_coupling": normal_values(splits[12], (GROUPS, COUPLING_RANK, TOP_SOURCES * COUPLING_RANK), (TOP_SOURCES * COUPLING_RANK) ** -0.5, 0.375, ((0, 64),)),
    }


def near_kernel(leaf_cluster_index, block_list, block_live, target_pts, source_pts, leaf_total):
    leaf_gap = (jnp.mod(leaf_cluster_index[:, None] - block_list + leaf_total // 2, leaf_total) - leaf_total // 2).astype(jnp.int32)
    leaf_gap = leaf_gap.astype(jnp.float32)
    target_f = target_pts.astype(jnp.float32)
    source_f = source_pts.astype(jnp.float32)
    across = float(NEAR_REACH)
    gap_x = leaf_gap[:, :, None, None] + target_f[:, None, 0, :, None] - source_f[:, :, 0, None, :]
    gap_y = across * (target_f[:, None, 1, :, None] - source_f[:, :, 1, None, :])
    gap_z = across * (target_f[:, None, 2, :, None] - source_f[:, :, 2, None, :])
    squared = gap_x * gap_x + gap_y * gap_y + gap_z * gap_z + 0.25
    slot_ids = jnp.arange(block_list.shape[1], dtype=jnp.int32)
    live_mask = (slot_ids[None, :] < block_live[:, None]).astype(jnp.float32)
    kernel = lax.rsqrt(squared * float(target_pts.shape[-1])) * live_mask[:, :, None, None]
    return kernel.astype(jnp.bfloat16)

def reference(charges, points, near_list, near_count, basis, far_list, leaf_coupling_stack, transfer, node_list, node_coupling, lift, top_list, top_coupling):
    leaf_total = charges.shape[0]
    right_sides = charges.shape[1]
    leaf_pts = charges.shape[2]
    rank_size = basis.shape[1]
    block_count = leaf_total // 64
    leaf_cluster_index = jnp.arange(leaf_total, dtype=jnp.int32)

    def moment_block(inputs_block):
        block_charges, block_basis = inputs_block
        return jnp.einsum('trp,tkp->trk', block_charges.astype(jnp.float32), block_basis.astype(jnp.float32)).astype(jnp.bfloat16)
    multipole_moments = lax.map(moment_block, (charges.reshape(block_count, 64, right_sides, leaf_pts), basis.reshape(block_count, 64, rank_size, leaf_pts)))
    multipole_moments = multipole_moments.reshape(leaf_total, right_sides, rank_size)
    far_count = far_list.shape[1]

    def leaf_block(inputs_block):
        block_ids, block_list, block_live, block_far, block_coupling = inputs_block
        kernel = near_kernel(block_ids, block_list, block_live, points[block_ids], points[block_list], leaf_total)
        near_part = jnp.einsum('tjip,tjrp->tri', kernel.astype(jnp.float32), charges[block_list].astype(jnp.float32))
        far_moments = multipole_moments[block_far].astype(jnp.float32)
        coupled = jnp.einsum('tjrq,tkjq->trk', far_moments, block_coupling.reshape(64, rank_size, far_count, rank_size).astype(jnp.float32))
        return (near_part, coupled)
    near_part, coupled = lax.map(leaf_block, (leaf_cluster_index.reshape(block_count, 64), near_list.reshape(block_count, 64, -1), near_count.reshape(block_count, 64), far_list.reshape(block_count, 64, far_count), leaf_coupling_stack.reshape(block_count, 64, rank_size, far_count * rank_size)))
    near_part = near_part.reshape(leaf_total, right_sides, leaf_pts)
    coupled = coupled.reshape(leaf_total, right_sides, rank_size)
    node_total = transfer.shape[0]
    leaves_per = leaf_total // node_total
    transfer_f = transfer.reshape(node_total, rank_size, leaves_per, rank_size).astype(jnp.float32)
    node_moment = jnp.einsum('ntrq,nktq->nrk', multipole_moments.reshape(node_total, leaves_per, right_sides, rank_size).astype(jnp.float32), transfer_f).astype(jnp.bfloat16)
    groups = top_coupling.shape[0]
    per_group = node_total // groups
    node_ids = jnp.arange(node_total, dtype=jnp.int32)
    source_nodes = ((node_ids // per_group)[:, None] * per_group + node_list).astype(jnp.int32)
    node_sources = node_list.shape[1]
    group_local = jnp.einsum('njrq,nkjq->nrk', node_moment[source_nodes].astype(jnp.float32), node_coupling.reshape(node_total, rank_size, node_sources, rank_size).astype(jnp.float32))
    lift_f = lift.astype(jnp.float32)
    grouped = node_moment.reshape(groups, per_group, right_sides, rank_size).astype(jnp.float32)
    top_moment = jnp.einsum('gsrq,gskq->grk', grouped, lift_f).astype(jnp.bfloat16)
    top_sources = top_list.shape[1]
    top_local = jnp.einsum('gjrq,gkjq->grk', top_moment[top_list].astype(jnp.float32), top_coupling.reshape(groups, rank_size, top_sources, rank_size).astype(jnp.float32)).astype(jnp.bfloat16)
    lifted = jnp.einsum('grk,gskq->gsrq', top_local.astype(jnp.float32), lift_f).reshape(node_total, right_sides, rank_size)
    resident_node_rows = (lifted + group_local).astype(jnp.bfloat16)
    broadcast_expansion = jnp.einsum('nrk,nktq->ntrq', resident_node_rows.astype(jnp.float32), transfer_f).reshape(leaf_total, right_sides, rank_size)
    leaf_local = (broadcast_expansion + coupled).astype(jnp.bfloat16)

    def final_block(inputs_block):
        block_local, block_basis, block_near = inputs_block
        far_part = jnp.einsum('trk,tkp->trp', block_local.astype(jnp.float32), block_basis.astype(jnp.float32))
        return (block_near + far_part).astype(jnp.bfloat16)
    potentials = lax.map(final_block, (leaf_local.reshape(block_count, 64, right_sides, rank_size), basis.reshape(block_count, 64, rank_size, leaf_pts), near_part.reshape(block_count, 64, right_sides, leaf_pts)))
    return potentials.reshape(leaf_total, right_sides, leaf_pts)
```

```python
import functools

import jax
import jax.numpy as jnp
from jax import lax
from jax.experimental import pallas as pl
from jax.experimental.pallas import tpu as pltpu
from jax.sharding import PartitionSpec as P

NEAR = 12
FAR = 20
EARLY = 6
BF = jnp.bfloat16
F = jnp.float32
MESH = pl.DeviceIdType.MESH
CONTRACT_LAST = (((1,), (1,)), ((), ()))


def dot_t(a, b):
    return lax.dot_general(a, b, CONTRACT_LAST, preferred_element_type=F)


def twice(x):
    return jnp.concatenate([x, x], axis=1)


def kernel(
    total, near_list, near_count, far_list, node_list, top_list,
    charges, points, basis, coupling, transfer, node_coupling, lift, top_coupling,
    out,
    ext_ch, ext_pt, ext_mo, fine, src_ch, rows, tiles, near_acc, spread, coupled,
    basis_v, coupling_v, transfer_v, ncoup_v, lift_v, tcoup_v, group_nm, top_own, top_all, top_part,
    load_sem, halo_send, halo_recv, nm_send, nm_recv, tm_send, tm_recv, tl_send, tl_recv,
):
    leaves = charges.shape[0]
    slots = near_list.shape[0]
    members = group_nm.shape[0]
    quarter, kinds = top_all.shape[0], top_part.shape[0]
    groups = quarter * kinds
    share = groups // members
    rank = ext_mo.shape[2] // 2
    g = lax.axis_index("leaf")
    e = lax.axis_index("grp")
    first = (g * members + e) * leaves
    right = (lax.rem(g + (e + 1) // members, groups), lax.rem(e + 1, members))
    left = (
        lax.rem(g + groups - 1 + (e + members - 1) // members, groups),
        lax.rem(e + members - 1, members),
    )
    kind = lax.rem(e, kinds)
    own_kind = lax.rem(g, kinds)
    catcher = (g // quarter) * kinds
    is_catcher = e // kinds == g // quarter
    target_member = (e // kinds) * kinds + own_kind

    loads = [
        pltpu.make_async_copy(src, dst, load_sem.at[i])
        for i, (src, dst) in enumerate(
            [
                (charges, ext_ch.at[pl.ds(NEAR, leaves)]),
                (basis, basis_v),
                (transfer, transfer_v),
                (lift, lift_v),
                (coupling, coupling_v),
                (node_coupling, ncoup_v),
                (top_coupling, tcoup_v),
            ]
        )
    ]
    for load in loads[:3]:
        load.start()

    barrier = pltpu.get_barrier_semaphore()

    def greet(device):
        pl.semaphore_signal(barrier, inc=1, device_id=device, device_id_type=MESH)

    @pl.when(is_catcher)
    def _():
        def greet_group(i, carry):
            peer = i * kinds + kind

            @pl.when(peer != g)
            def _():
                greet((peer, g // share))

            return carry

        lax.fori_loop(0, quarter, greet_group, 0)

    greet(right)
    greet(left)

    def greet_member(i, carry):
        greet((g, lax.rem(e + i, members)))
        return carry

    lax.fori_loop(1, members, greet_member, 0)
    for load in loads[3:]:
        load.start()

    loads[0].wait()
    loads[1].wait()

    def moment(t, carry):
        b = basis_v[t]
        m = dot_t(ext_ch[NEAR + t], jnp.concatenate([b, b], 0))
        ext_mo[FAR + t] = m.astype(BF)
        return carry

    lax.fori_loop(0, leaves, moment, 0, unroll=8)
    lane = lax.broadcasted_iota(jnp.int32, (ext_mo.shape[1], ext_mo.shape[2]), 1)
    low = lane < rank

    def pair(a, b):
        return jnp.where(low, a, b)

    loads[2].wait()
    packed = [pair(ext_mo[FAR + 2 * u], ext_mo[FAR + 2 * u + 1]) for u in range(leaves // 2)]
    own_nm = dot_t(jnp.concatenate(packed, 1), transfer_v[0])
    group_nm[e] = twice(own_nm).astype(BF)

    fine[...] = points[...].astype(F)
    pad = jnp.zeros((13, points.shape[2]), F)

    def own_points(t, carry):
        p = jnp.concatenate([fine[c, pl.ds(t, 1), :] for c in range(3)] + [pad], 0)
        ext_pt[NEAR + t] = p.astype(BF)
        return carry

    lax.fori_loop(0, leaves, own_points, 0, unroll=4)

    def own_tiles(t, carry):
        cols = ext_pt[NEAR + t].astype(F)[:8].T
        for c in range(3):
            tiles[t, c] = jnp.broadcast_to(cols[:, c : c + 1], tiles.shape[2:]).astype(BF)
        return carry

    def sources(s, carry):
        p = ext_pt[s].astype(F)
        for c in range(3):
            rows[s, c] = jnp.broadcast_to(p[c : c + 1], p.shape).astype(BF)
        src_ch[s] = ext_ch[s]
        return carry

    def no_source(s, carry):
        src_ch[s] = jnp.zeros_like(src_ch[s])
        rows[s] = jnp.zeros_like(rows[s])
        return carry

    scale = F(1.0 / (NEAR * points.shape[2] ** 0.5))
    inverse = BF(1.0 / NEAR**2)
    soft = BF(0.25 / NEAR**2)
    copies = tiles.shape[2] // rows.shape[2]

    def tall(row):
        return jnp.concatenate([row] * copies, 0)

    def near(t, carry):
        acc = jnp.zeros(near_acc.shape[1:], F)
        count = near_count[t]
        for j0 in range(0, slots, 2):
            ks = []
            cs = []
            for j in (j0, j0 + 1):
                s = lax.rem(near_list[j, t] - first + NEAR + total, total)
                s = jnp.clip(s, 0, rows.shape[0] - 1)
                gap = (t + NEAR - s).astype(F).astype(BF)
                dx = tiles[t, 0] - tall(rows[s, 0] - gap)
                dy = tiles[t, 1] - tall(rows[s, 1])
                dz = tiles[t, 2] - tall(rows[s, 2])
                square = dx * dx * inverse + soft + (dy * dy + dz * dz)
                ks.append(lax.rsqrt(square))
                live = jnp.where(j < count, F(1), F(0)).astype(BF)
                cs.append(src_ch[s] * live)
            acc = acc + dot_t(jnp.concatenate(cs, 1), jnp.concatenate(ks, 1))
        near_acc[t] = acc * scale
        return carry

    def near_inner():
        lax.fori_loop(0, leaves, own_tiles, 0, unroll=2)
        lax.fori_loop(0, NEAR, no_source, 0, unroll=4)
        lax.fori_loop(NEAR + leaves, leaves + 2 * NEAR, no_source, 0, unroll=4)
        lax.fori_loop(NEAR, NEAR + leaves, sources, 0, unroll=4)
        lax.fori_loop(NEAR, leaves - NEAR, near, 0, unroll=2)

    ahead = lax.rem(g, groups // 2) < groups // EARLY
    pl.when(ahead)(near_inner)

    begin = e * share
    mine = jnp.logical_and(g >= begin, g < begin + share)
    targets = jnp.where(mine, share - 1, share)
    pl.semaphore_wait(barrier, 2 + (members - 1) + targets)

    def nm_copy(i):
        peer = lax.rem(e + i, members)
        return pltpu.make_async_remote_copy(
            src_ref=group_nm.at[e],
            dst_ref=group_nm.at[e],
            send_sem=nm_send.at[peer],
            recv_sem=nm_recv.at[e],
            device_id=(g, peer),
            device_id_type=MESH,
        )

    def nm_start(i, carry):
        nm_copy(i).start()
        return carry

    lax.fori_loop(1, members, nm_start, 0)

    to_right = []
    to_left = []
    for i, (buf, width) in enumerate([(ext_ch, NEAR), (ext_pt, NEAR), (ext_mo, FAR)]):
        to_right.append(
            pltpu.make_async_remote_copy(
                src_ref=buf.at[pl.ds(leaves, width)],
                dst_ref=buf.at[pl.ds(0, width)],
                send_sem=halo_send.at[2 * i],
                recv_sem=halo_recv.at[2 * i],
                device_id=right,
                device_id_type=MESH,
            )
        )
        to_left.append(
            pltpu.make_async_remote_copy(
                src_ref=buf.at[pl.ds(width, width)],
                dst_ref=buf.at[pl.ds(leaves + width, width)],
                send_sem=halo_send.at[2 * i + 1],
                recv_sem=halo_recv.at[2 * i + 1],
                device_id=left,
                device_id_type=MESH,
            )
        )
    for i in range(3):
        to_right[i].start()
        to_left[i].start()

    loads[3].wait()

    def nm_done(i, carry):
        peer = lax.rem(e + i, members)
        pltpu.make_async_remote_copy(
            src_ref=group_nm.at[peer],
            dst_ref=group_nm.at[peer],
            send_sem=nm_send.at[peer],
            recv_sem=nm_recv.at[peer],
            device_id=(g, peer),
            device_id_type=MESH,
        ).wait()
        return carry

    lax.fori_loop(1, members, nm_done, 0)
    top = jnp.zeros((group_nm.shape[1], rank), F)
    for i in range(members):
        top = top + dot_t(group_nm[i][:, :rank], lift_v[0, i])
    top_own[...] = twice(top).astype(BF)

    @pl.when(jnp.logical_and(is_catcher, kind == own_kind))
    def _():
        top_all[g // kinds] = top_own[...]


    def tm_copy(i):
        return pltpu.make_async_remote_copy(
            src_ref=top_own,
            dst_ref=top_all.at[g // kinds],
            send_sem=tm_send.at[i],
            recv_sem=tm_recv.at[g // kinds],
            device_id=(e * share + i, target_member),
            device_id_type=MESH,
        )

    for i in range(share):

        @pl.when(e * share + i != g)
        def _(i=i):
            tm_copy(i).start()

    pl.when(jnp.logical_not(ahead))(near_inner)
    for i in range(2):
        to_left[i].wait_recv()
    lax.fori_loop(NEAR + leaves, leaves + 2 * NEAR, sources, 0, unroll=4)
    lax.fori_loop(leaves - NEAR, leaves, near, 0, unroll=2)
    for i in range(2):
        to_right[i].wait_recv()
    lax.fori_loop(0, NEAR, sources, 0, unroll=4)
    lax.fori_loop(0, NEAR, near, 0, unroll=2)

    loads[4].wait()
    to_left[2].wait_recv()
    to_right[2].wait_recv()

    def couple(t, carry):
        m = []
        for j in range(far_list.shape[0]):
            s = lax.rem(far_list[j, t] - first + FAR + total, total)
            m.append(ext_mo[jnp.clip(s, 0, ext_mo.shape[0] - 1)])
        lhs = [pair(m[j], m[j + 1]) for j in range(0, len(m), 2)]
        coupled[t] = dot_t(jnp.concatenate(lhs, 1), coupling_v[t])
        return carry

    lax.fori_loop(0, leaves, couple, 0, unroll=8)
    loads[5].wait()
    nodes = pair(group_nm[node_list[0, 0]], group_nm[node_list[0, 1]])
    group_local = dot_t(nodes, ncoup_v[0])

    loads[6].wait()

    def part_copy(i):
        return pltpu.make_async_remote_copy(
            src_ref=top_part.at[kind],
            dst_ref=top_part.at[kind],
            send_sem=tl_send.at[i],
            recv_sem=tl_recv.at[kind],
            device_id=(g, lax.rem(e + i, members)),
            device_id_type=MESH,
        )

    @pl.when(is_catcher)
    def _():
        def tm_done(i, carry):
            peer = i * kinds + kind

            @pl.when(peer != g)
            def _():
                pltpu.make_async_remote_copy(
                    src_ref=top_all.at[i],
                    dst_ref=top_all.at[i],
                    send_sem=tm_send.at[0],
                    recv_sem=tm_recv.at[i],
                    device_id=(peer, g // share),
                    device_id_type=MESH,
                ).wait_recv()

            return carry

        lax.fori_loop(0, quarter, tm_done, 0)
        terms = []
        for j in range(top_list.shape[1]):
            source = top_list[0, j]
            here = jnp.where(lax.rem(source, kinds) == kind, F(1), F(0)).astype(BF)
            terms.append(top_all[jnp.clip(source // kinds, 0, quarter - 1)] * here)
        lhs = [pair(terms[j], terms[j + 1]) for j in range(0, len(terms), 2)]
        top_part[kind] = twice(dot_t(jnp.concatenate(lhs, 1), tcoup_v[0]))

        def part_start(i, carry):
            part_copy(i).start()
            return carry

        lax.fori_loop(1, members, part_start, 0)

    for k in range(kinds):

        @pl.when(catcher + k != e)
        def _(k=k):
            pltpu.make_async_remote_copy(
                src_ref=top_part.at[k],
                dst_ref=top_part.at[k],
                send_sem=tl_send.at[0],
                recv_sem=tl_recv.at[k],
                device_id=(g, catcher + k),
                device_id_type=MESH,
            ).wait_recv()

    top_local = jnp.sum(top_part[...], axis=0)[:, :rank].astype(BF)
    resident = group_local + jnp.dot(top_local, lift_v[0, e], preferred_element_type=F)
    wide = jnp.dot(resident.astype(BF), transfer_v[0], preferred_element_type=F)
    for u in range(leaves // 2):
        spread[u] = wide[:, 2 * rank * u : 2 * rank * (u + 1)]

    def finish(u, carry):
        base = spread[u]
        for h in range(2):
            t = 2 * u + h
            local = (coupled[t] + base[:, rank * h : rank * (h + 1)]).astype(BF)
            far = jnp.dot(local, basis_v[t], preferred_element_type=F)
            out[t] = (near_acc[t] + far).astype(out.dtype)
        return carry

    lax.fori_loop(0, leaves // 2, finish, 0, unroll=4)

    for h in to_right + to_left:
        h.wait_send()
    for i in range(share):

        @pl.when(e * share + i != g)
        def _(i=i):
            tm_copy(i).wait_send()

    @pl.when(is_catcher)
    def _():
        def part_sent(i, carry):
            part_copy(i).wait_send()
            return carry

        lax.fori_loop(1, members, part_sent, 0)


def shards(
    charges, points, near_list, near_count, basis, far_list, coupling, transfer, node_list,
    node_coupling, lift, top_list, top_coupling,
):
    leaves, right_sides, leaf_pts = charges.shape
    rank = basis.shape[1]
    members = lax.axis_size("grp")
    groups = lax.axis_size("leaf")
    share = groups // members
    kinds = 4
    smem = pl.BlockSpec(memory_space=pltpu.SMEM)
    vmem = pl.BlockSpec(memory_space=pltpu.VMEM)
    hbm = pl.BlockSpec(memory_space=pl.ANY)
    scratch = [
        pltpu.VMEM((leaves + 2 * NEAR, right_sides, leaf_pts), BF),
        pltpu.VMEM((leaves + 2 * NEAR, 16, leaf_pts), BF),
        pltpu.VMEM((leaves + 2 * FAR, right_sides, 2 * rank), BF),
        pltpu.VMEM((3, leaves, leaf_pts), F),
        pltpu.VMEM((leaves + 2 * NEAR, right_sides, leaf_pts), BF),
        pltpu.VMEM((leaves + 2 * NEAR, 3, 16, leaf_pts), BF),
        pltpu.VMEM((leaves, 3, leaf_pts, leaf_pts), BF),
        pltpu.VMEM((leaves, right_sides, leaf_pts), F),
        pltpu.VMEM((leaves // 2, right_sides, 2 * rank), F),
        pltpu.VMEM((leaves, right_sides, rank), F),
        pltpu.VMEM(basis.shape, BF),
        pltpu.VMEM(coupling.shape, BF),
        pltpu.VMEM(transfer.shape, BF),
        pltpu.VMEM(node_coupling.shape, BF),
        pltpu.VMEM(lift.shape, BF),
        pltpu.VMEM(top_coupling.shape, BF),
        pltpu.VMEM((members, right_sides, 2 * rank), BF),
        pltpu.VMEM((right_sides, 2 * rank), BF),
        pltpu.VMEM((groups // kinds, right_sides, 2 * rank), BF),
        pltpu.VMEM((kinds, right_sides, 2 * rank), F),
        pltpu.SemaphoreType.DMA((7,)),
        pltpu.SemaphoreType.DMA((6,)),
        pltpu.SemaphoreType.DMA((6,)),
        pltpu.SemaphoreType.DMA((members,)),
        pltpu.SemaphoreType.DMA((members,)),
        pltpu.SemaphoreType.DMA((share,)),
        pltpu.SemaphoreType.DMA((groups // kinds,)),
        pltpu.SemaphoreType.DMA((members,)),
        pltpu.SemaphoreType.DMA((kinds,)),
    ]
    result = pl.pallas_call(
        functools.partial(kernel, leaves * members * groups),
        out_shape=jax.ShapeDtypeStruct((leaves, right_sides, leaf_pts), F),
        in_specs=[smem] * 5 + [hbm, vmem] + [hbm] * 6,
        out_specs=vmem,
        scratch_shapes=scratch,
        compiler_params=pltpu.CompilerParams(
            collective_id=0, has_side_effects=True, vmem_limit_bytes=56 * 2**20
        ),
    )(
        near_list.T, near_count, far_list.T, node_list, top_list, charges, points.transpose(1, 0, 2), basis, coupling,
        transfer, node_coupling, lift, top_coupling,
    )
    return result.astype(BF)


def solution(mesh):
    both = ("leaf", "grp")
    return jax.shard_map(
        shards,
        mesh=mesh,
        in_specs=(
            P(both, None, None),
            P(both, None, None),
            P(both, None),
            P(both),
            P(both, None, None),
            P(both, None),
            P(both, None, None),
            P(both, None, None),
            P(both, None),
            P(both, None, None),
            P("leaf", None, None, None),
            P("leaf", None),
            P("leaf", None, None),
        ),
        out_specs=P(both, None, None),
        check_vma=False,
    )
```

```python
import functools

import jax
import jax.numpy as jnp
from jax import lax
from jax.experimental import pallas as pl
from jax.experimental.pallas import tpu as pltpu
from jax.sharding import PartitionSpec as P

NEAR = 12
FAR = 20
EARLY = 4
BF = jnp.bfloat16
F = jnp.float32
MESH = pl.DeviceIdType.MESH
CONTRACT_LAST = (((1,), (1,)), ((), ()))


def dot_t(a, b):
    return lax.dot_general(a, b, CONTRACT_LAST, preferred_element_type=F)


def twice(x):
    return jnp.concatenate([x, x], axis=1)


def kernel(
    total, near_list, near_count, far_list, node_list, top_list,
    charges, points, basis, coupling, transfer, node_coupling, lift, top_coupling,
    out,
    ext_ch, ext_pt, ext_mo, fine, src_ch, rows, tiles, near_acc, spread, coupled, group_loc,
    basis_v, coupling_v, transfer_v, ncoup_v, lift_v, tcoup_v, group_nm, top_own, top_all, top_part,
    load_sem, halo_send, halo_recv, nm_send, nm_recv, tm_send, tm_recv, tl_send, tl_recv,
):
    leaves = charges.shape[0]
    slots = near_list.shape[0]
    members = group_nm.shape[0]
    quarter, kinds = top_all.shape[0], top_part.shape[0]
    groups = quarter * kinds
    share = groups // members
    rank = ext_mo.shape[2] // 2
    g = lax.axis_index("leaf")
    e = lax.axis_index("grp")
    first = (g * members + e) * leaves
    right = (lax.rem(g + (e + 1) // members, groups), lax.rem(e + 1, members))
    left = (
        lax.rem(g + groups - 1 + (e + members - 1) // members, groups),
        lax.rem(e + members - 1, members),
    )
    kind = lax.rem(e, kinds)
    own_kind = lax.rem(g, kinds)
    catcher = (g // quarter) * kinds
    is_catcher = e // kinds == g // quarter
    target_member = (e // kinds) * kinds + own_kind

    loads = [
        pltpu.make_async_copy(src, dst, load_sem.at[i])
        for i, (src, dst) in enumerate(
            [
                (charges, ext_ch.at[pl.ds(NEAR, leaves)]),
                (basis, basis_v),
                (transfer, transfer_v),
                (lift, lift_v),
                (coupling, coupling_v),
                (node_coupling, ncoup_v),
                (top_coupling, tcoup_v),
            ]
        )
    ]
    for load in loads[:3]:
        load.start()

    barrier = pltpu.get_barrier_semaphore()

    def greet(device):
        pl.semaphore_signal(barrier, inc=1, device_id=device, device_id_type=MESH)

    @pl.when(is_catcher)
    def _():
        def greet_group(i, carry):
            peer = i * kinds + kind

            @pl.when(peer != g)
            def _():
                greet((peer, g // share))

            return carry

        lax.fori_loop(0, quarter, greet_group, 0)

    greet(right)
    greet(left)

    def greet_member(i, carry):
        greet((g, lax.rem(e + i, members)))
        return carry

    lax.fori_loop(1, members, greet_member, 0)
    for load in loads[3:]:
        load.start()

    loads[0].wait()
    loads[1].wait()

    def moment(t, carry):
        b = basis_v[t]
        m = dot_t(ext_ch[NEAR + t], jnp.concatenate([b, b], 0))
        ext_mo[FAR + t] = m.astype(BF)
        return carry

    lax.fori_loop(0, leaves, moment, 0, unroll=8)
    lane = lax.broadcasted_iota(jnp.int32, (ext_mo.shape[1], ext_mo.shape[2]), 1)
    low = lane < rank

    def pair(a, b):
        return jnp.where(low, a, b)

    loads[2].wait()
    packed = [pair(ext_mo[FAR + 2 * u], ext_mo[FAR + 2 * u + 1]) for u in range(leaves // 2)]
    own_nm = dot_t(jnp.concatenate(packed, 1), transfer_v[0])
    group_nm[e] = twice(own_nm).astype(BF)

    fine[...] = points[...].astype(F)
    pad = jnp.zeros((13, points.shape[2]), F)

    def own_points(t, carry):
        p = jnp.concatenate([fine[c, pl.ds(t, 1), :] for c in range(3)] + [pad], 0)
        ext_pt[NEAR + t] = p.astype(BF)
        return carry

    lax.fori_loop(0, leaves, own_points, 0, unroll=4)

    def own_tiles(t, carry):
        cols = ext_pt[NEAR + t].astype(F)[:8].T
        for c in range(3):
            tiles[t, c] = jnp.broadcast_to(cols[:, c : c + 1], tiles.shape[2:]).astype(BF)
        return carry

    def sources(s, carry):
        p = ext_pt[s].astype(F)
        for c in range(3):
            rows[s, c] = jnp.broadcast_to(p[c : c + 1], p.shape).astype(BF)
        src_ch[s] = ext_ch[s]
        return carry

    def no_source(s, carry):
        src_ch[s] = jnp.zeros_like(src_ch[s])
        rows[s] = jnp.zeros_like(rows[s])
        return carry

    scale = F(1.0 / (NEAR * points.shape[2] ** 0.5))
    inverse = BF(1.0 / NEAR**2)
    soft = BF(0.25 / NEAR**2)
    copies = tiles.shape[2] // rows.shape[2]

    def tall(row):
        return jnp.concatenate([row] * copies, 0)

    def near(t, carry):
        acc = jnp.zeros(near_acc.shape[1:], F)
        count = near_count[t]
        for j0 in range(0, slots, 2):
            ks = []
            cs = []
            for j in (j0, j0 + 1):
                s = lax.rem(near_list[j, t] - first + NEAR + total, total)
                s = jnp.clip(s, 0, rows.shape[0] - 1)
                gap = (t + NEAR - s).astype(F).astype(BF)
                dx = tiles[t, 0] - tall(rows[s, 0] - gap)
                dy = tiles[t, 1] - tall(rows[s, 1])
                dz = tiles[t, 2] - tall(rows[s, 2])
                square = dx * dx * inverse + soft + (dy * dy + dz * dz)
                ks.append(lax.rsqrt(square))
                live = jnp.where(j < count, F(1), F(0)).astype(BF)
                cs.append(src_ch[s] * live)
            acc = acc + dot_t(jnp.concatenate(cs, 1), jnp.concatenate(ks, 1))
        near_acc[t] = acc * scale
        return carry

    def near_pair(u, carry):
        near(2 * u, carry)
        return near(2 * u + 1, carry)

    ahead = lax.rem(g, groups // 2) < groups // EARLY
    lax.fori_loop(0, leaves, own_tiles, 0, unroll=2)
    lax.fori_loop(0, NEAR, no_source, 0, unroll=4)
    lax.fori_loop(NEAR + leaves, leaves + 2 * NEAR, no_source, 0, unroll=4)
    lax.fori_loop(NEAR, NEAR + leaves, sources, 0, unroll=4)

    def nm_copy(i):
        peer = lax.rem(e + i, members)
        return pltpu.make_async_remote_copy(
            src_ref=group_nm.at[e],
            dst_ref=group_nm.at[e],
            send_sem=nm_send.at[peer],
            recv_sem=nm_recv.at[e],
            device_id=(g, peer),
            device_id_type=MESH,
        )

    to_right = []
    to_left = []
    for i, (buf, width) in enumerate([(ext_ch, NEAR), (ext_pt, NEAR), (ext_mo, FAR)]):
        to_right.append(
            pltpu.make_async_remote_copy(
                src_ref=buf.at[pl.ds(leaves, width)],
                dst_ref=buf.at[pl.ds(0, width)],
                send_sem=halo_send.at[2 * i],
                recv_sem=halo_recv.at[2 * i],
                device_id=right,
                device_id_type=MESH,
            )
        )
        to_left.append(
            pltpu.make_async_remote_copy(
                src_ref=buf.at[pl.ds(width, width)],
                dst_ref=buf.at[pl.ds(leaves + width, width)],
                send_sem=halo_send.at[2 * i + 1],
                recv_sem=halo_recv.at[2 * i + 1],
                device_id=left,
                device_id_type=MESH,
            )
        )
    def tm_copy(i):
        return pltpu.make_async_remote_copy(
            src_ref=top_own,
            dst_ref=top_all.at[g // kinds],
            send_sem=tm_send.at[i],
            recv_sem=tm_recv.at[g // kinds],
            device_id=(e * share + i, target_member),
            device_id_type=MESH,
        )

    def part_copy(i):
        return pltpu.make_async_remote_copy(
            src_ref=top_part.at[kind],
            dst_ref=top_part.at[kind],
            send_sem=tl_send.at[i],
            recv_sem=tl_recv.at[kind],
            device_id=(g, lax.rem(e + i, members)),
            device_id_type=MESH,
        )

    def enter():
        begin = e * share
        mine = jnp.logical_and(g >= begin, g < begin + share)
        targets = jnp.where(mine, share - 1, share)
        pl.semaphore_wait(barrier, 2 + (members - 1) + targets)

        def nm_start(i, carry):
            nm_copy(i).start()
            return carry

        lax.fori_loop(1, members, nm_start, 0)

        for i in range(3):
            to_right[i].start()
            to_left[i].start()

    def lift_group():
        loads[3].wait()

        def nm_done(i, carry):
            peer = lax.rem(e + i, members)
            pltpu.make_async_remote_copy(
                src_ref=group_nm.at[peer],
                dst_ref=group_nm.at[peer],
                send_sem=nm_send.at[peer],
                recv_sem=nm_recv.at[peer],
                device_id=(g, peer),
                device_id_type=MESH,
            ).wait()
            return carry

        lax.fori_loop(1, members, nm_done, 0)
        top = jnp.zeros((group_nm.shape[1], rank), F)
        for i in range(members):
            top = top + dot_t(group_nm[i][:, :rank], lift_v[0, i])
        top_own[...] = twice(top).astype(BF)

        @pl.when(jnp.logical_and(is_catcher, kind == own_kind))
        def _():
            top_all[g // kinds] = top_own[...]


        for i in range(share):

            @pl.when(e * share + i != g)
            def _(i=i):
                tm_copy(i).start()

    def from_right():
        for i in range(2):
            to_left[i].wait_recv()
        lax.fori_loop(NEAR + leaves, leaves + 2 * NEAR, sources, 0, unroll=4)

    def hand_on():
        loads[4].wait()
        to_left[2].wait_recv()
        to_right[2].wait_recv()

        def couple(t, carry):
            m = []
            for j in range(far_list.shape[0]):
                s = lax.rem(far_list[j, t] - first + FAR + total, total)
                m.append(ext_mo[jnp.clip(s, 0, ext_mo.shape[0] - 1)])
            lhs = [pair(m[j], m[j + 1]) for j in range(0, len(m), 2)]
            coupled[t] = dot_t(jnp.concatenate(lhs, 1), coupling_v[t])
            return carry

        lax.fori_loop(0, leaves, couple, 0, unroll=8)
        loads[5].wait()
        nodes = pair(group_nm[node_list[0, 0]], group_nm[node_list[0, 1]])
        group_loc[...] = dot_t(nodes, ncoup_v[0])

        loads[6].wait()

        @pl.when(is_catcher)
        def _():
            def tm_done(i, carry):
                peer = i * kinds + kind

                @pl.when(peer != g)
                def _():
                    pltpu.make_async_remote_copy(
                        src_ref=top_all.at[i],
                        dst_ref=top_all.at[i],
                        send_sem=tm_send.at[0],
                        recv_sem=tm_recv.at[i],
                        device_id=(peer, g // share),
                        device_id_type=MESH,
                    ).wait_recv()

                return carry

            lax.fori_loop(0, quarter, tm_done, 0)
            terms = []
            for j in range(top_list.shape[1]):
                source = top_list[0, j]
                here = jnp.where(lax.rem(source, kinds) == kind, F(1), F(0)).astype(BF)
                terms.append(top_all[jnp.clip(source // kinds, 0, quarter - 1)] * here)
            lhs = [pair(terms[j], terms[j + 1]) for j in range(0, len(terms), 2)]
            top_part[kind] = twice(dot_t(jnp.concatenate(lhs, 1), tcoup_v[0]))

            def part_start(i, carry):
                part_copy(i).start()
                return carry

            lax.fori_loop(1, members, part_start, 0)

        for i in range(2):
            to_right[i].wait_recv()
        lax.fori_loop(0, NEAR, sources, 0, unroll=4)

    edge = NEAR // 2
    inner = leaves // 2 - 2 * edge
    half = inner // 2
    free = jnp.where(ahead, inner, 0)
    steps = [
        (None, edge, free),
        (enter, edge, jnp.where(ahead, 0, half)),
        (lift_group, edge + half, jnp.where(ahead, 0, inner - half)),
        (from_right, edge + inner, edge),
        (hand_on, 0, edge),
    ]

    def phase(p, carry):
        begin = 0
        size = 0
        for i, (step, start, count) in enumerate(steps):
            if step is not None:
                pl.when(p == i)(step)
            begin = jnp.where(p == i, start, begin)
            size = jnp.where(p == i, count, size)
        lax.fori_loop(begin, begin + size, near_pair, 0)
        return carry

    lax.fori_loop(0, len(steps), phase, 0)

    for k in range(kinds):

        @pl.when(catcher + k != e)
        def _(k=k):
            pltpu.make_async_remote_copy(
                src_ref=top_part.at[k],
                dst_ref=top_part.at[k],
                send_sem=tl_send.at[0],
                recv_sem=tl_recv.at[k],
                device_id=(g, catcher + k),
                device_id_type=MESH,
            ).wait_recv()

    top_local = jnp.sum(top_part[...], axis=0)[:, :rank].astype(BF)
    resident = group_loc[...] + jnp.dot(top_local, lift_v[0, e], preferred_element_type=F)
    wide = jnp.dot(resident.astype(BF), transfer_v[0], preferred_element_type=F)
    for u in range(leaves // 2):
        spread[u] = wide[:, 2 * rank * u : 2 * rank * (u + 1)]

    def finish(u, carry):
        base = spread[u]
        for h in range(2):
            t = 2 * u + h
            local = (coupled[t] + base[:, rank * h : rank * (h + 1)]).astype(BF)
            far = jnp.dot(local, basis_v[t], preferred_element_type=F)
            out[t] = (near_acc[t] + far).astype(out.dtype)
        return carry

    lax.fori_loop(0, leaves // 2, finish, 0, unroll=4)

    for h in to_right + to_left:
        h.wait_send()
    for i in range(share):

        @pl.when(e * share + i != g)
        def _(i=i):
            tm_copy(i).wait_send()

    @pl.when(is_catcher)
    def _():
        def part_sent(i, carry):
            part_copy(i).wait_send()
            return carry

        lax.fori_loop(1, members, part_sent, 0)


def shards(
    charges, points, near_list, near_count, basis, far_list, coupling, transfer, node_list,
    node_coupling, lift, top_list, top_coupling,
):
    leaves, right_sides, leaf_pts = charges.shape
    rank = basis.shape[1]
    members = lax.axis_size("grp")
    groups = lax.axis_size("leaf")
    share = groups // members
    kinds = 4
    smem = pl.BlockSpec(memory_space=pltpu.SMEM)
    vmem = pl.BlockSpec(memory_space=pltpu.VMEM)
    hbm = pl.BlockSpec(memory_space=pl.ANY)
    scratch = [
        pltpu.VMEM((leaves + 2 * NEAR, right_sides, leaf_pts), BF),
        pltpu.VMEM((leaves + 2 * NEAR, 16, leaf_pts), BF),
        pltpu.VMEM((leaves + 2 * FAR, right_sides, 2 * rank), BF),
        pltpu.VMEM((3, leaves, leaf_pts), F),
        pltpu.VMEM((leaves + 2 * NEAR, right_sides, leaf_pts), BF),
        pltpu.VMEM((leaves + 2 * NEAR, 3, 16, leaf_pts), BF),
        pltpu.VMEM((leaves, 3, leaf_pts, leaf_pts), BF),
        pltpu.VMEM((leaves, right_sides, leaf_pts), F),
        pltpu.VMEM((leaves // 2, right_sides, 2 * rank), F),
        pltpu.VMEM((leaves, right_sides, rank), F),
        pltpu.VMEM((right_sides, rank), F),
        pltpu.VMEM(basis.shape, BF),
        pltpu.VMEM(coupling.shape, BF),
        pltpu.VMEM(transfer.shape, BF),
        pltpu.VMEM(node_coupling.shape, BF),
        pltpu.VMEM(lift.shape, BF),
        pltpu.VMEM(top_coupling.shape, BF),
        pltpu.VMEM((members, right_sides, 2 * rank), BF),
        pltpu.VMEM((right_sides, 2 * rank), BF),
        pltpu.VMEM((groups // kinds, right_sides, 2 * rank), BF),
        pltpu.VMEM((kinds, right_sides, 2 * rank), F),
        pltpu.SemaphoreType.DMA((7,)),
        pltpu.SemaphoreType.DMA((6,)),
        pltpu.SemaphoreType.DMA((6,)),
        pltpu.SemaphoreType.DMA((members,)),
        pltpu.SemaphoreType.DMA((members,)),
        pltpu.SemaphoreType.DMA((share,)),
        pltpu.SemaphoreType.DMA((groups // kinds,)),
        pltpu.SemaphoreType.DMA((members,)),
        pltpu.SemaphoreType.DMA((kinds,)),
    ]
    result = pl.pallas_call(
        functools.partial(kernel, leaves * members * groups),
        out_shape=jax.ShapeDtypeStruct((leaves, right_sides, leaf_pts), F),
        in_specs=[smem] * 5 + [hbm, vmem] + [hbm] * 6,
        out_specs=vmem,
        scratch_shapes=scratch,
        compiler_params=pltpu.CompilerParams(
            collective_id=0, has_side_effects=True, vmem_limit_bytes=56 * 2**20
        ),
    )(
        near_list.T, near_count, far_list.T, node_list, top_list, charges, points.transpose(1, 0, 2), basis, coupling,
        transfer, node_coupling, lift, top_coupling,
    )
    return result.astype(BF)


def solution(mesh):
    both = ("leaf", "grp")
    return jax.shard_map(
        shards,
        mesh=mesh,
        in_specs=(
            P(both, None, None),
            P(both, None, None),
            P(both, None),
            P(both),
            P(both, None, None),
            P(both, None),
            P(both, None, None),
            P(both, None, None),
            P(both, None),
            P(both, None, None),
            P("leaf", None, None, None),
            P("leaf", None),
            P("leaf", None, None),
        ),
        out_specs=P(both, None, None),
        check_vma=False,
    )
```

```python
import functools

import jax
import jax.numpy as jnp
from jax import lax
from jax.experimental import pallas as pl
from jax.experimental.pallas import tpu as pltpu
from jax.sharding import PartitionSpec as P

NEAR = 12
FAR = 20
EARLY = 4
BF = jnp.bfloat16
F = jnp.float32
MESH = pl.DeviceIdType.MESH
CONTRACT_LAST = (((1,), (1,)), ((), ()))


def dot_t(a, b):
    return lax.dot_general(a, b, CONTRACT_LAST, preferred_element_type=F)


def twice(x):
    return jnp.concatenate([x, x], axis=1)


def kernel(
    total, near_list, near_count, far_list, node_list, top_list,
    charges, points, basis, coupling, transfer, node_coupling, lift, top_coupling,
    out,
    ext_ch, ext_pt, ext_mo, fine, src_ch, rows, tiles, near_acc, spread, coupled, group_loc,
    basis_v, coupling_v, transfer_v, ncoup_v, lift_v, tcoup_v, group_nm, top_own, top_all, top_part,
    load_sem, halo_send, halo_recv, nm_send, nm_recv, tm_send, tm_recv, tl_send, tl_recv,
):
    leaves = charges.shape[0]
    slots = near_list.shape[0]
    members = group_nm.shape[0]
    quarter, kinds = top_all.shape[0], top_part.shape[0]
    groups = quarter * kinds
    share = groups // members
    rank = ext_mo.shape[2] // 2
    g = lax.axis_index("leaf")
    e = lax.axis_index("grp")
    first = (g * members + e) * leaves
    right = (lax.rem(g + (e + 1) // members, groups), lax.rem(e + 1, members))
    left = (
        lax.rem(g + groups - 1 + (e + members - 1) // members, groups),
        lax.rem(e + members - 1, members),
    )
    kind = lax.rem(e, kinds)
    own_kind = lax.rem(g, kinds)
    catcher = (g // quarter) * kinds
    is_catcher = e // kinds == g // quarter
    target_member = (e // kinds) * kinds + own_kind

    loads = [
        pltpu.make_async_copy(src, dst, load_sem.at[i])
        for i, (src, dst) in enumerate(
            [
                (charges, ext_ch.at[pl.ds(NEAR, leaves)]),
                (basis, basis_v),
                (transfer, transfer_v),
                (lift, lift_v),
                (coupling, coupling_v),
                (node_coupling, ncoup_v),
                (top_coupling, tcoup_v),
            ]
        )
    ]
    for load in loads[:3]:
        load.start()

    barrier = pltpu.get_barrier_semaphore()

    def greet(device):
        pl.semaphore_signal(barrier, inc=1, device_id=device, device_id_type=MESH)

    @pl.when(is_catcher)
    def _():
        def greet_group(i, carry):
            peer = i * kinds + kind

            @pl.when(peer != g)
            def _():
                greet((peer, g // share))

            return carry

        lax.fori_loop(0, quarter, greet_group, 0)

    greet(right)
    greet(left)

    def greet_member(i, carry):
        greet((g, lax.rem(e + i, members)))
        return carry

    lax.fori_loop(1, members, greet_member, 0)
    for load in loads[3:]:
        load.start()

    loads[0].wait()
    loads[1].wait()

    def moment(t, carry):
        b = basis_v[t]
        m = dot_t(ext_ch[NEAR + t], jnp.concatenate([b, b], 0))
        ext_mo[FAR + t] = m.astype(BF)
        return carry

    lax.fori_loop(0, leaves, moment, 0, unroll=8)
    lane = lax.broadcasted_iota(jnp.int32, (ext_mo.shape[1], ext_mo.shape[2]), 1)
    low = lane < rank

    def pair(a, b):
        return jnp.where(low, a, b)

    loads[2].wait()
    packed = [pair(ext_mo[FAR + 2 * u], ext_mo[FAR + 2 * u + 1]) for u in range(leaves // 2)]
    own_nm = dot_t(jnp.concatenate(packed, 1), transfer_v[0])
    group_nm[e] = twice(own_nm).astype(BF)

    fine[...] = points[...].astype(F)
    pad = jnp.zeros((13, points.shape[2]), F)

    def own_points(t, carry):
        p = jnp.concatenate([fine[c, pl.ds(t, 1), :] for c in range(3)] + [pad], 0)
        ext_pt[NEAR + t] = p.astype(BF)
        return carry

    lax.fori_loop(0, leaves, own_points, 0, unroll=4)

    def own_tiles(t, carry):
        cols = ext_pt[NEAR + t].astype(F)[:8].T
        for c in range(3):
            tiles[t, c] = jnp.broadcast_to(cols[:, c : c + 1], tiles.shape[2:]).astype(BF)
        return carry

    def sources(s, carry):
        p = ext_pt[s].astype(F)
        for c in range(3):
            rows[s, c] = jnp.broadcast_to(p[c : c + 1], p.shape).astype(BF)
        src_ch[s] = ext_ch[s]
        return carry

    def no_source(s, carry):
        src_ch[s] = jnp.zeros_like(src_ch[s])
        rows[s] = jnp.zeros_like(rows[s])
        return carry

    scale = F(1.0 / (NEAR * points.shape[2] ** 0.5))
    inverse = BF(1.0 / NEAR**2)
    soft = BF(0.25 / NEAR**2)
    copies = tiles.shape[2] // rows.shape[2]

    def tall(row):
        return jnp.concatenate([row] * copies, 0)

    def near(t, carry):
        acc = jnp.zeros(near_acc.shape[1:], F)
        count = near_count[t]
        for j0 in range(0, slots, 2):
            ks = []
            cs = []
            for j in (j0, j0 + 1):
                s = lax.rem(near_list[j, t] - first + NEAR + total, total)
                s = jnp.clip(s, 0, rows.shape[0] - 1)
                gap = (t + NEAR - s).astype(F).astype(BF)
                dx = tiles[t, 0] - tall(rows[s, 0] - gap)
                dy = tiles[t, 1] - tall(rows[s, 1])
                dz = tiles[t, 2] - tall(rows[s, 2])
                square = dx * dx * inverse + soft + (dy * dy + dz * dz)
                ks.append(lax.rsqrt(square))
                live = jnp.where(j < count, F(1), F(0)).astype(BF)
                cs.append(src_ch[s] * live)
            acc = acc + dot_t(jnp.concatenate(cs, 1), jnp.concatenate(ks, 1))
        near_acc[t] = acc * scale
        return carry

    def near_pair(u, carry):
        near(2 * u, carry)
        return near(2 * u + 1, carry)

    ahead = lax.rem(g, groups // 2) < groups // EARLY
    def prepare_tiles():
        lax.fori_loop(0, leaves, own_tiles, 0, unroll=2)

    def prepare_sources():
        lax.fori_loop(0, NEAR, no_source, 0, unroll=4)
        lax.fori_loop(NEAR + leaves, leaves + 2 * NEAR, no_source, 0, unroll=4)
        lax.fori_loop(NEAR, NEAR + leaves, sources, 0, unroll=4)

    def nm_copy(i):
        peer = lax.rem(e + i, members)
        return pltpu.make_async_remote_copy(
            src_ref=group_nm.at[e],
            dst_ref=group_nm.at[e],
            send_sem=nm_send.at[peer],
            recv_sem=nm_recv.at[e],
            device_id=(g, peer),
            device_id_type=MESH,
        )

    to_right = []
    to_left = []
    for i, (buf, width) in enumerate([(ext_ch, NEAR), (ext_pt, NEAR), (ext_mo, FAR)]):
        to_right.append(
            pltpu.make_async_remote_copy(
                src_ref=buf.at[pl.ds(leaves, width)],
                dst_ref=buf.at[pl.ds(0, width)],
                send_sem=halo_send.at[2 * i],
                recv_sem=halo_recv.at[2 * i],
                device_id=right,
                device_id_type=MESH,
            )
        )
        to_left.append(
            pltpu.make_async_remote_copy(
                src_ref=buf.at[pl.ds(width, width)],
                dst_ref=buf.at[pl.ds(leaves + width, width)],
                send_sem=halo_send.at[2 * i + 1],
                recv_sem=halo_recv.at[2 * i + 1],
                device_id=left,
                device_id_type=MESH,
            )
        )
    def tm_copy(i):
        return pltpu.make_async_remote_copy(
            src_ref=top_own,
            dst_ref=top_all.at[g // kinds],
            send_sem=tm_send.at[i],
            recv_sem=tm_recv.at[g // kinds],
            device_id=(e * share + i, target_member),
            device_id_type=MESH,
        )

    def part_copy(i):
        return pltpu.make_async_remote_copy(
            src_ref=top_part.at[kind],
            dst_ref=top_part.at[kind],
            send_sem=tl_send.at[i],
            recv_sem=tl_recv.at[kind],
            device_id=(g, lax.rem(e + i, members)),
            device_id_type=MESH,
        )

    def enter():
        begin = e * share
        mine = jnp.logical_and(g >= begin, g < begin + share)
        targets = jnp.where(mine, share - 1, share)
        pl.semaphore_wait(barrier, 2 + (members - 1) + targets)

        def nm_start(i, carry):
            nm_copy(i).start()
            return carry

        lax.fori_loop(1, members, nm_start, 0)

        for i in range(3):
            to_right[i].start()
            to_left[i].start()

    def lift_group():
        loads[3].wait()

        def nm_done(i, carry):
            peer = lax.rem(e + i, members)
            pltpu.make_async_remote_copy(
                src_ref=group_nm.at[peer],
                dst_ref=group_nm.at[peer],
                send_sem=nm_send.at[peer],
                recv_sem=nm_recv.at[peer],
                device_id=(g, peer),
                device_id_type=MESH,
            ).wait()
            return carry

        lax.fori_loop(1, members, nm_done, 0)
        top = jnp.zeros((group_nm.shape[1], rank), F)
        for i in range(members):
            top = top + dot_t(group_nm[i][:, :rank], lift_v[0, i])
        top_own[...] = twice(top).astype(BF)

        @pl.when(jnp.logical_and(is_catcher, kind == own_kind))
        def _():
            top_all[g // kinds] = top_own[...]


        for i in range(share):

            @pl.when(e * share + i != g)
            def _(i=i):
                tm_copy(i).start()

    def from_right():
        for i in range(2):
            to_left[i].wait_recv()
        lax.fori_loop(NEAR + leaves, leaves + 2 * NEAR, sources, 0, unroll=4)

    def hand_on():
        loads[4].wait()
        to_left[2].wait_recv()
        to_right[2].wait_recv()

        def couple(t, carry):
            m = []
            for j in range(far_list.shape[0]):
                s = lax.rem(far_list[j, t] - first + FAR + total, total)
                m.append(ext_mo[jnp.clip(s, 0, ext_mo.shape[0] - 1)])
            lhs = [pair(m[j], m[j + 1]) for j in range(0, len(m), 2)]
            coupled[t] = dot_t(jnp.concatenate(lhs, 1), coupling_v[t])
            return carry

        lax.fori_loop(0, leaves, couple, 0, unroll=8)
        loads[5].wait()
        nodes = pair(group_nm[node_list[0, 0]], group_nm[node_list[0, 1]])
        group_loc[...] = dot_t(nodes, ncoup_v[0])

        loads[6].wait()

        @pl.when(is_catcher)
        def _():
            def tm_done(i, carry):
                peer = i * kinds + kind

                @pl.when(peer != g)
                def _():
                    pltpu.make_async_remote_copy(
                        src_ref=top_all.at[i],
                        dst_ref=top_all.at[i],
                        send_sem=tm_send.at[0],
                        recv_sem=tm_recv.at[i],
                        device_id=(peer, g // share),
                        device_id_type=MESH,
                    ).wait_recv()

                return carry

            lax.fori_loop(0, quarter, tm_done, 0)
            terms = []
            for j in range(top_list.shape[1]):
                source = top_list[0, j]
                here = jnp.where(lax.rem(source, kinds) == kind, F(1), F(0)).astype(BF)
                terms.append(top_all[jnp.clip(source // kinds, 0, quarter - 1)] * here)
            lhs = [pair(terms[j], terms[j + 1]) for j in range(0, len(terms), 2)]
            top_part[kind] = twice(dot_t(jnp.concatenate(lhs, 1), tcoup_v[0]))

            def part_start(i, carry):
                part_copy(i).start()
                return carry

            lax.fori_loop(1, members, part_start, 0)

    def from_left():
        for i in range(2):
            to_right[i].wait_recv()
        lax.fori_loop(0, NEAR, sources, 0, unroll=4)

    edge = NEAR // 2
    inner = leaves // 2 - 2 * edge
    late = jnp.logical_not(ahead)
    phases = [
        ([(prepare_tiles, ahead), (prepare_sources, ahead)], edge, jnp.where(ahead, inner, 0)),
        ([(enter, None), (prepare_tiles, late)], edge, 0),
        ([(lift_group, late), (prepare_sources, late)], edge, jnp.where(ahead, 0, inner)),
        ([(from_right, None)], edge + inner, edge),
        ([(lift_group, ahead), (from_left, None)], 0, edge // 2),
        ([(hand_on, None)], edge // 2, edge - edge // 2),
    ]

    def phase(p, carry):
        def run(step):
            now = jnp.bool_(False)
            for i, (steps, _, _) in enumerate(phases):
                for other, when in steps:
                    if other is step:
                        here = p == i
                        if when is not None:
                            here = jnp.logical_and(here, when)
                        now = jnp.logical_or(now, here)
            pl.when(now)(step)

        for step in (enter, prepare_tiles, lift_group, prepare_sources, from_right, from_left, hand_on):
            run(step)
        begin = 0
        size = 0
        for i, (_, start, count) in enumerate(phases):
            begin = jnp.where(p == i, start, begin)
            size = jnp.where(p == i, count, size)
        lax.fori_loop(begin, begin + size, near_pair, 0)
        return carry

    lax.fori_loop(0, len(phases), phase, 0)

    for k in range(kinds):

        @pl.when(catcher + k != e)
        def _(k=k):
            pltpu.make_async_remote_copy(
                src_ref=top_part.at[k],
                dst_ref=top_part.at[k],
                send_sem=tl_send.at[0],
                recv_sem=tl_recv.at[k],
                device_id=(g, catcher + k),
                device_id_type=MESH,
            ).wait_recv()

    top_local = jnp.sum(top_part[...], axis=0)[:, :rank].astype(BF)
    resident = group_loc[...] + jnp.dot(top_local, lift_v[0, e], preferred_element_type=F)
    wide = jnp.dot(resident.astype(BF), transfer_v[0], preferred_element_type=F)
    for u in range(leaves // 2):
        spread[u] = wide[:, 2 * rank * u : 2 * rank * (u + 1)]

    def finish(u, carry):
        base = spread[u]
        for h in range(2):
            t = 2 * u + h
            local = (coupled[t] + base[:, rank * h : rank * (h + 1)]).astype(BF)
            far = jnp.dot(local, basis_v[t], preferred_element_type=F)
            out[t] = (near_acc[t] + far).astype(out.dtype)
        return carry

    lax.fori_loop(0, leaves // 2, finish, 0, unroll=8)

    for h in to_right + to_left:
        h.wait_send()
    for i in range(share):

        @pl.when(e * share + i != g)
        def _(i=i):
            tm_copy(i).wait_send()

    @pl.when(is_catcher)
    def _():
        def part_sent(i, carry):
            part_copy(i).wait_send()
            return carry

        lax.fori_loop(1, members, part_sent, 0)


def shards(
    charges, points, near_list, near_count, basis, far_list, coupling, transfer, node_list,
    node_coupling, lift, top_list, top_coupling,
):
    leaves, right_sides, leaf_pts = charges.shape
    rank = basis.shape[1]
    members = lax.axis_size("grp")
    groups = lax.axis_size("leaf")
    share = groups // members
    kinds = 4
    smem = pl.BlockSpec(memory_space=pltpu.SMEM)
    vmem = pl.BlockSpec(memory_space=pltpu.VMEM)
    hbm = pl.BlockSpec(memory_space=pl.ANY)
    scratch = [
        pltpu.VMEM((leaves + 2 * NEAR, right_sides, leaf_pts), BF),
        pltpu.VMEM((leaves + 2 * NEAR, 16, leaf_pts), BF),
        pltpu.VMEM((leaves + 2 * FAR, right_sides, 2 * rank), BF),
        pltpu.VMEM((3, leaves, leaf_pts), F),
        pltpu.VMEM((leaves + 2 * NEAR, right_sides, leaf_pts), BF),
        pltpu.VMEM((leaves + 2 * NEAR, 3, 16, leaf_pts), BF),
        pltpu.VMEM((leaves, 3, leaf_pts, leaf_pts), BF),
        pltpu.VMEM((leaves, right_sides, leaf_pts), F),
        pltpu.VMEM((leaves // 2, right_sides, 2 * rank), F),
        pltpu.VMEM((leaves, right_sides, rank), F),
        pltpu.VMEM((right_sides, rank), F),
        pltpu.VMEM(basis.shape, BF),
        pltpu.VMEM(coupling.shape, BF),
        pltpu.VMEM(transfer.shape, BF),
        pltpu.VMEM(node_coupling.shape, BF),
        pltpu.VMEM(lift.shape, BF),
        pltpu.VMEM(top_coupling.shape, BF),
        pltpu.VMEM((members, right_sides, 2 * rank), BF),
        pltpu.VMEM((right_sides, 2 * rank), BF),
        pltpu.VMEM((groups // kinds, right_sides, 2 * rank), BF),
        pltpu.VMEM((kinds, right_sides, 2 * rank), F),
        pltpu.SemaphoreType.DMA((7,)),
        pltpu.SemaphoreType.DMA((6,)),
        pltpu.SemaphoreType.DMA((6,)),
        pltpu.SemaphoreType.DMA((members,)),
        pltpu.SemaphoreType.DMA((members,)),
        pltpu.SemaphoreType.DMA((share,)),
        pltpu.SemaphoreType.DMA((groups // kinds,)),
        pltpu.SemaphoreType.DMA((members,)),
        pltpu.SemaphoreType.DMA((kinds,)),
    ]
    result = pl.pallas_call(
        functools.partial(kernel, leaves * members * groups),
        out_shape=jax.ShapeDtypeStruct((leaves, right_sides, leaf_pts), BF),
        in_specs=[smem] * 5 + [hbm, vmem] + [hbm] * 6,
        out_specs=vmem,
        scratch_shapes=scratch,
        compiler_params=pltpu.CompilerParams(
            collective_id=0, has_side_effects=True, vmem_limit_bytes=56 * 2**20
        ),
    )(
        near_list.T, near_count, far_list.T, node_list, top_list, charges, points.transpose(1, 0, 2), basis, coupling,
        transfer, node_coupling, lift, top_coupling,
    )
    return result


def solution(mesh):
    both = ("leaf", "grp")
    return jax.shard_map(
        shards,
        mesh=mesh,
        in_specs=(
            P(both, None, None),
            P(both, None, None),
            P(both, None),
            P(both),
            P(both, None, None),
            P(both, None),
            P(both, None, None),
            P(both, None, None),
            P(both, None),
            P(both, None, None),
            P("leaf", None, None, None),
            P("leaf", None),
            P("leaf", None, None),
        ),
        out_specs=P(both, None, None),
        check_vma=False,
    )
```

```python
import functools

import jax
import jax.numpy as jnp
from jax import lax
from jax.experimental import pallas as pl
from jax.experimental.pallas import tpu as pltpu
from jax.sharding import PartitionSpec as P

NEAR = 12
FAR = 20
EARLY = 4
BF = jnp.bfloat16
F = jnp.float32
MESH = pl.DeviceIdType.MESH
CONTRACT_LAST = (((1,), (1,)), ((), ()))


def dot_t(a, b):
    return lax.dot_general(a, b, CONTRACT_LAST, preferred_element_type=F)


def twice(x):
    return jnp.concatenate([x, x], axis=1)


def kernel(
    total, near_list, near_count, far_list, node_list, top_list,
    charges, points, basis, coupling, transfer, node_coupling, lift, top_coupling,
    out,
    ext_ch, ext_pt, ext_mo, fine, src_ch, rows, tiles, near_acc, spread, coupled, group_loc,
    basis_v, coupling_v, transfer_v, ncoup_v, lift_v, tcoup_v, group_nm, top_own, top_all, top_part,
    load_sem, halo_send, halo_recv, nm_send, nm_recv, tm_send, tm_recv, tl_send, tl_recv,
):
    leaves = charges.shape[0]
    slots = near_list.shape[0]
    members = group_nm.shape[0]
    quarter, kinds = top_all.shape[0], top_part.shape[0]
    groups = quarter * kinds
    share = groups // members
    rank = ext_mo.shape[2] // 2
    g = lax.axis_index("leaf")
    e = lax.axis_index("grp")
    first = (g * members + e) * leaves
    right = (lax.rem(g + (e + 1) // members, groups), lax.rem(e + 1, members))
    left = (
        lax.rem(g + groups - 1 + (e + members - 1) // members, groups),
        lax.rem(e + members - 1, members),
    )
    kind = lax.rem(e, kinds)
    own_kind = lax.rem(g, kinds)
    catcher = (g // quarter) * kinds
    is_catcher = e // kinds == g // quarter
    target_member = (e // kinds) * kinds + own_kind

    loads = [
        pltpu.make_async_copy(src, dst, load_sem.at[i])
        for i, (src, dst) in enumerate(
            [
                (charges, ext_ch.at[pl.ds(NEAR, leaves)]),
                (basis, basis_v),
                (transfer, transfer_v),
                (lift, lift_v),
                (coupling, coupling_v),
                (node_coupling, ncoup_v),
                (top_coupling, tcoup_v),
            ]
        )
    ]
    for load in loads[:3]:
        load.start()

    barrier = pltpu.get_barrier_semaphore()

    def greet(device):
        pl.semaphore_signal(barrier, inc=1, device_id=device, device_id_type=MESH)

    @pl.when(is_catcher)
    def _():
        def greet_group(i, carry):
            peer = i * kinds + kind

            @pl.when(peer != g)
            def _():
                greet((peer, g // share))

            return carry

        lax.fori_loop(0, quarter, greet_group, 0)

    greet(right)
    greet(left)

    def greet_member(i, carry):
        greet((g, lax.rem(e + i, members)))
        return carry

    lax.fori_loop(1, members, greet_member, 0)
    for load in loads[3:]:
        load.start()

    loads[0].wait()
    loads[1].wait()

    def moment(t, carry):
        b = basis_v[t]
        m = dot_t(ext_ch[NEAR + t], jnp.concatenate([b, b], 0))
        ext_mo[FAR + t] = m.astype(BF)
        return carry

    lax.fori_loop(0, leaves, moment, 0, unroll=8)
    lane = lax.broadcasted_iota(jnp.int32, (ext_mo.shape[1], ext_mo.shape[2]), 1)
    low = lane < rank

    def pair(a, b):
        return jnp.where(low, a, b)

    loads[2].wait()
    packed = [pair(ext_mo[FAR + 2 * u], ext_mo[FAR + 2 * u + 1]) for u in range(leaves // 2)]
    own_nm = dot_t(jnp.concatenate(packed, 1), transfer_v[0])
    group_nm[e] = twice(own_nm).astype(BF)

    fine[...] = points[...].astype(F)
    pad = jnp.zeros((13, points.shape[2]), F)

    def own_points(t, carry):
        p = jnp.concatenate([fine[c, pl.ds(t, 1), :] for c in range(3)] + [pad], 0)
        ext_pt[NEAR + t] = p.astype(BF)
        return carry

    lax.fori_loop(0, leaves, own_points, 0, unroll=4)

    def own_tiles(t, carry):
        cols = ext_pt[NEAR + t].astype(F)[:8].T
        for c in range(3):
            tiles[t, c] = jnp.broadcast_to(cols[:, c : c + 1], tiles.shape[2:]).astype(BF)
        return carry

    def sources(s, carry):
        p = ext_pt[s].astype(F)
        for c in range(3):
            rows[s, c] = jnp.broadcast_to(p[c : c + 1], p.shape).astype(BF)
        src_ch[s] = ext_ch[s]
        return carry

    def no_source(s, carry):
        src_ch[s] = jnp.zeros_like(src_ch[s])
        rows[s] = jnp.zeros_like(rows[s])
        return carry

    scale = F(1.0 / (NEAR * points.shape[2] ** 0.5))
    inverse = BF(1.0 / NEAR**2)
    soft = BF(0.25 / NEAR**2)
    copies = tiles.shape[2] // rows.shape[2]

    def tall(row):
        return jnp.concatenate([row] * copies, 0)

    def near(t, carry):
        acc = jnp.zeros(near_acc.shape[1:], F)
        count = near_count[t]
        for j0 in range(0, slots, 2):
            ks = []
            cs = []
            for j in (j0, j0 + 1):
                s = lax.rem(near_list[j, t] - first + NEAR + total, total)
                s = jnp.clip(s, 0, rows.shape[0] - 1)
                gap = (t + NEAR - s).astype(F).astype(BF)
                dx = tiles[t, 0] - tall(rows[s, 0] - gap)
                dy = tiles[t, 1] - tall(rows[s, 1])
                dz = tiles[t, 2] - tall(rows[s, 2])
                square = dx * dx * inverse + soft + (dy * dy + dz * dz)
                ks.append(lax.rsqrt(square))
                live = jnp.where(j < count, F(1), F(0)).astype(BF)
                cs.append(src_ch[s] * live)
            acc = acc + dot_t(jnp.concatenate(cs, 1), jnp.concatenate(ks, 1))
        near_acc[t] = acc * scale
        return carry

    def near_four(u, carry):
        for i in range(4):
            near(4 * u + i, carry)
        return carry

    ahead = lax.rem(g, groups // 2) < groups // EARLY
    lax.fori_loop(0, leaves, own_tiles, 0, unroll=2)
    lax.fori_loop(0, NEAR, no_source, 0, unroll=4)
    lax.fori_loop(NEAR + leaves, leaves + 2 * NEAR, no_source, 0, unroll=4)
    lax.fori_loop(NEAR, NEAR + leaves, sources, 0, unroll=4)

    def nm_copy(i):
        peer = lax.rem(e + i, members)
        return pltpu.make_async_remote_copy(
            src_ref=group_nm.at[e],
            dst_ref=group_nm.at[e],
            send_sem=nm_send.at[peer],
            recv_sem=nm_recv.at[e],
            device_id=(g, peer),
            device_id_type=MESH,
        )

    to_right = []
    to_left = []
    for i, (buf, width) in enumerate([(ext_ch, NEAR), (ext_pt, NEAR), (ext_mo, FAR)]):
        to_right.append(
            pltpu.make_async_remote_copy(
                src_ref=buf.at[pl.ds(leaves, width)],
                dst_ref=buf.at[pl.ds(0, width)],
                send_sem=halo_send.at[2 * i],
                recv_sem=halo_recv.at[2 * i],
                device_id=right,
                device_id_type=MESH,
            )
        )
        to_left.append(
            pltpu.make_async_remote_copy(
                src_ref=buf.at[pl.ds(width, width)],
                dst_ref=buf.at[pl.ds(leaves + width, width)],
                send_sem=halo_send.at[2 * i + 1],
                recv_sem=halo_recv.at[2 * i + 1],
                device_id=left,
                device_id_type=MESH,
            )
        )
    def tm_copy(i):
        return pltpu.make_async_remote_copy(
            src_ref=top_own,
            dst_ref=top_all.at[g // kinds],
            send_sem=tm_send.at[i],
            recv_sem=tm_recv.at[g // kinds],
            device_id=(e * share + i, target_member),
            device_id_type=MESH,
        )

    def part_copy(i):
        return pltpu.make_async_remote_copy(
            src_ref=top_part.at[kind],
            dst_ref=top_part.at[kind],
            send_sem=tl_send.at[i],
            recv_sem=tl_recv.at[kind],
            device_id=(g, lax.rem(e + i, members)),
            device_id_type=MESH,
        )

    def enter():
        begin = e * share
        mine = jnp.logical_and(g >= begin, g < begin + share)
        targets = jnp.where(mine, share - 1, share)
        pl.semaphore_wait(barrier, 2 + (members - 1) + targets)

        def nm_start(i, carry):
            nm_copy(i).start()
            return carry

        lax.fori_loop(1, members, nm_start, 0)

        for i in range(3):
            to_right[i].start()
            to_left[i].start()

    def lift_group():
        loads[3].wait()

        def nm_done(i, carry):
            peer = lax.rem(e + i, members)
            pltpu.make_async_remote_copy(
                src_ref=group_nm.at[peer],
                dst_ref=group_nm.at[peer],
                send_sem=nm_send.at[peer],
                recv_sem=nm_recv.at[peer],
                device_id=(g, peer),
                device_id_type=MESH,
            ).wait()
            return carry

        lax.fori_loop(1, members, nm_done, 0)
        top = jnp.zeros((group_nm.shape[1], rank), F)
        for i in range(members):
            top = top + dot_t(group_nm[i][:, :rank], lift_v[0, i])
        top_own[...] = twice(top).astype(BF)

        @pl.when(jnp.logical_and(is_catcher, kind == own_kind))
        def _():
            top_all[g // kinds] = top_own[...]


        for i in range(share):

            @pl.when(e * share + i != g)
            def _(i=i):
                tm_copy(i).start()

    def from_right():
        for i in range(2):
            to_left[i].wait_recv()
        lax.fori_loop(NEAR + leaves, leaves + 2 * NEAR, sources, 0, unroll=4)

    def hand_on():
        loads[4].wait()
        to_left[2].wait_recv()
        to_right[2].wait_recv()

        def couple(t, carry):
            m = []
            for j in range(far_list.shape[0]):
                s = lax.rem(far_list[j, t] - first + FAR + total, total)
                m.append(ext_mo[jnp.clip(s, 0, ext_mo.shape[0] - 1)])
            lhs = [pair(m[j], m[j + 1]) for j in range(0, len(m), 2)]
            coupled[t] = dot_t(jnp.concatenate(lhs, 1), coupling_v[t])
            return carry

        lax.fori_loop(0, leaves, couple, 0, unroll=8)
        loads[5].wait()
        nodes = pair(group_nm[node_list[0, 0]], group_nm[node_list[0, 1]])
        group_loc[...] = dot_t(nodes, ncoup_v[0])

        loads[6].wait()

        @pl.when(is_catcher)
        def _():
            def tm_done(i, carry):
                peer = i * kinds + kind

                @pl.when(peer != g)
                def _():
                    pltpu.make_async_remote_copy(
                        src_ref=top_all.at[i],
                        dst_ref=top_all.at[i],
                        send_sem=tm_send.at[0],
                        recv_sem=tm_recv.at[i],
                        device_id=(peer, g // share),
                        device_id_type=MESH,
                    ).wait_recv()

                return carry

            lax.fori_loop(0, quarter, tm_done, 0)
            terms = []
            for j in range(top_list.shape[1]):
                source = top_list[0, j]
                here = jnp.where(lax.rem(source, kinds) == kind, F(1), F(0)).astype(BF)
                terms.append(top_all[jnp.clip(source // kinds, 0, quarter - 1)] * here)
            lhs = [pair(terms[j], terms[j + 1]) for j in range(0, len(terms), 2)]
            top_part[kind] = twice(dot_t(jnp.concatenate(lhs, 1), tcoup_v[0]))

            def part_start(i, carry):
                part_copy(i).start()
                return carry

            lax.fori_loop(1, members, part_start, 0)

        for i in range(2):
            to_right[i].wait_recv()
        lax.fori_loop(0, NEAR, sources, 0, unroll=4)

    edge = NEAR // 4
    inner = leaves // 4 - 2 * edge
    half = inner // 2
    late = jnp.logical_not(ahead)

    def choose(a, b):
        return jnp.where(ahead, a, b)

    phases = [
        ([], edge, choose(inner, 0)),
        ([(enter, True), (from_right, ahead)], choose(edge + inner, edge), choose(1, half)),
        (
            [(lift_group, True)],
            choose(edge + inner + 1, edge + half),
            choose(edge - 1, inner - half),
        ),
        ([(from_right, late)], edge + inner, choose(0, edge)),
        ([(hand_on, True)], 0, edge),
    ]

    def phase(p, carry):
        for step in (enter, lift_group, from_right, hand_on):
            now = False
            for i, (steps, _, _) in enumerate(phases):
                for other, takes in steps:
                    if other is step:
                        now = jnp.logical_or(now, jnp.logical_and(p == i, takes))
            pl.when(now)(step)
        begin = 0
        size = 0
        for i, (_, start, count) in enumerate(phases):
            begin = jnp.where(p == i, start, begin)
            size = jnp.where(p == i, count, size)
        lax.fori_loop(begin, begin + size, near_four, 0)
        return carry

    lax.fori_loop(0, len(phases), phase, 0)

    for k in range(kinds):

        @pl.when(catcher + k != e)
        def _(k=k):
            pltpu.make_async_remote_copy(
                src_ref=top_part.at[k],
                dst_ref=top_part.at[k],
                send_sem=tl_send.at[0],
                recv_sem=tl_recv.at[k],
                device_id=(g, catcher + k),
                device_id_type=MESH,
            ).wait_recv()

    top_local = jnp.sum(top_part[...], axis=0)[:, :rank].astype(BF)
    resident = group_loc[...] + jnp.dot(top_local, lift_v[0, e], preferred_element_type=F)
    wide = jnp.dot(resident.astype(BF), transfer_v[0], preferred_element_type=F)
    for u in range(leaves // 2):
        spread[u] = wide[:, 2 * rank * u : 2 * rank * (u + 1)]

    def finish(u, carry):
        base = spread[u]
        for h in range(2):
            t = 2 * u + h
            local = (coupled[t] + base[:, rank * h : rank * (h + 1)]).astype(BF)
            far = jnp.dot(local, basis_v[t], preferred_element_type=F)
            out[t] = (near_acc[t] + far).astype(out.dtype)
        return carry

    lax.fori_loop(0, leaves // 2, finish, 0, unroll=8)

    for h in to_right + to_left:
        h.wait_send()
    for i in range(share):

        @pl.when(e * share + i != g)
        def _(i=i):
            tm_copy(i).wait_send()

    @pl.when(is_catcher)
    def _():
        def part_sent(i, carry):
            part_copy(i).wait_send()
            return carry

        lax.fori_loop(1, members, part_sent, 0)


def shards(
    charges, points, near_list, near_count, basis, far_list, coupling, transfer, node_list,
    node_coupling, lift, top_list, top_coupling,
):
    leaves, right_sides, leaf_pts = charges.shape
    rank = basis.shape[1]
    members = lax.axis_size("grp")
    groups = lax.axis_size("leaf")
    share = groups // members
    kinds = 4
    smem = pl.BlockSpec(memory_space=pltpu.SMEM)
    vmem = pl.BlockSpec(memory_space=pltpu.VMEM)
    hbm = pl.BlockSpec(memory_space=pl.ANY)
    scratch = [
        pltpu.VMEM((leaves + 2 * NEAR, right_sides, leaf_pts), BF),
        pltpu.VMEM((leaves + 2 * NEAR, 16, leaf_pts), BF),
        pltpu.VMEM((leaves + 2 * FAR, right_sides, 2 * rank), BF),
        pltpu.VMEM((3, leaves, leaf_pts), F),
        pltpu.VMEM((leaves + 2 * NEAR, right_sides, leaf_pts), BF),
        pltpu.VMEM((leaves + 2 * NEAR, 3, 16, leaf_pts), BF),
        pltpu.VMEM((leaves, 3, leaf_pts, leaf_pts), BF),
        pltpu.VMEM((leaves, right_sides, leaf_pts), F),
        pltpu.VMEM((leaves // 2, right_sides, 2 * rank), F),
        pltpu.VMEM((leaves, right_sides, rank), F),
        pltpu.VMEM((right_sides, rank), F),
        pltpu.VMEM(basis.shape, BF),
        pltpu.VMEM(coupling.shape, BF),
        pltpu.VMEM(transfer.shape, BF),
        pltpu.VMEM(node_coupling.shape, BF),
        pltpu.VMEM(lift.shape, BF),
        pltpu.VMEM(top_coupling.shape, BF),
        pltpu.VMEM((members, right_sides, 2 * rank), BF),
        pltpu.VMEM((right_sides, 2 * rank), BF),
        pltpu.VMEM((groups // kinds, right_sides, 2 * rank), BF),
        pltpu.VMEM((kinds, right_sides, 2 * rank), F),
        pltpu.SemaphoreType.DMA((7,)),
        pltpu.SemaphoreType.DMA((6,)),
        pltpu.SemaphoreType.DMA((6,)),
        pltpu.SemaphoreType.DMA((members,)),
        pltpu.SemaphoreType.DMA((members,)),
        pltpu.SemaphoreType.DMA((share,)),
        pltpu.SemaphoreType.DMA((groups // kinds,)),
        pltpu.SemaphoreType.DMA((members,)),
        pltpu.SemaphoreType.DMA((kinds,)),
    ]
    result = pl.pallas_call(
        functools.partial(kernel, leaves * members * groups),
        out_shape=jax.ShapeDtypeStruct((leaves, right_sides, leaf_pts), BF),
        in_specs=[smem] * 5 + [hbm, vmem] + [hbm] * 6,
        out_specs=vmem,
        scratch_shapes=scratch,
        compiler_params=pltpu.CompilerParams(
            collective_id=0, has_side_effects=True, vmem_limit_bytes=56 * 2**20
        ),
    )(
        near_list.T, near_count, far_list.T, node_list, top_list, charges, points.transpose(1, 0, 2), basis, coupling,
        transfer, node_coupling, lift, top_coupling,
    )
    return result


def solution(mesh):
    both = ("leaf", "grp")
    return jax.shard_map(
        shards,
        mesh=mesh,
        in_specs=(
            P(both, None, None),
            P(both, None, None),
            P(both, None),
            P(both),
            P(both, None, None),
            P(both, None),
            P(both, None, None),
            P(both, None, None),
            P(both, None),
            P(both, None, None),
            P("leaf", None, None, None),
            P("leaf", None),
            P("leaf", None, None),
        ),
        out_specs=P(both, None, None),
        check_vma=False,
    )
```

```python
import functools

import jax
import jax.numpy as jnp
from jax import lax
from jax.experimental import pallas as pl
from jax.experimental.pallas import tpu as pltpu
from jax.sharding import PartitionSpec as P

NEAR = 12
FAR = 20
EARLY = 4
BF = jnp.bfloat16
F = jnp.float32
MESH = pl.DeviceIdType.MESH
CONTRACT_LAST = (((1,), (1,)), ((), ()))


def dot_t(a, b):
    return lax.dot_general(a, b, CONTRACT_LAST, preferred_element_type=F)


def twice(x):
    return jnp.concatenate([x, x], axis=1)


def kernel(
    total, near_list, near_count, far_list, node_list, top_list,
    charges, points, basis, coupling, transfer, node_coupling, lift, top_coupling,
    out,
    ext_ch, ext_pt, ext_mo, fine, src_ch, rows, tiles, near_acc, spread, coupled, group_loc,
    basis_v, coupling_v, transfer_v, ncoup_v, lift_v, tcoup_v, group_nm, top_own, top_all, top_part,
    load_sem, halo_send, halo_recv, nm_send, nm_recv, tm_send, tm_recv, tl_send, tl_recv,
):
    leaves = charges.shape[0]
    slots = near_list.shape[0]
    members = group_nm.shape[0]
    quarter, kinds = top_all.shape[0], top_part.shape[0]
    groups = quarter * kinds
    share = groups // members
    rank = ext_mo.shape[2] // 2
    g = lax.axis_index("leaf")
    e = lax.axis_index("grp")
    first = (g * members + e) * leaves
    right = (lax.rem(g + (e + 1) // members, groups), lax.rem(e + 1, members))
    left = (
        lax.rem(g + groups - 1 + (e + members - 1) // members, groups),
        lax.rem(e + members - 1, members),
    )
    kind = lax.rem(e, kinds)
    own_kind = lax.rem(g, kinds)
    catcher = (g // quarter) * kinds
    is_catcher = e // kinds == g // quarter
    target_member = (e // kinds) * kinds + own_kind

    loads = [
        pltpu.make_async_copy(src, dst, load_sem.at[i])
        for i, (src, dst) in enumerate(
            [
                (charges, ext_ch.at[pl.ds(NEAR, leaves)]),
                (basis, basis_v),
                (transfer, transfer_v),
                (lift, lift_v),
                (coupling, coupling_v),
                (node_coupling, ncoup_v),
                (top_coupling, tcoup_v),
            ]
        )
    ]
    for load in loads[:3]:
        load.start()

    barrier = pltpu.get_barrier_semaphore()

    def greet(device):
        pl.semaphore_signal(barrier, inc=1, device_id=device, device_id_type=MESH)

    @pl.when(is_catcher)
    def _():
        def greet_group(i, carry):
            peer = i * kinds + kind

            @pl.when(peer != g)
            def _():
                greet((peer, g // share))

            return carry

        lax.fori_loop(0, quarter, greet_group, 0)

    greet(right)
    greet(left)

    def greet_member(i, carry):
        greet((g, lax.rem(e + i, members)))
        return carry

    lax.fori_loop(1, members, greet_member, 0)
    for load in loads[3:]:
        load.start()

    loads[0].wait()
    loads[1].wait()

    def moment(t, carry):
        b = basis_v[t]
        m = dot_t(ext_ch[NEAR + t], jnp.concatenate([b, b], 0))
        ext_mo[FAR + t] = m.astype(BF)
        return carry

    lax.fori_loop(0, leaves, moment, 0, unroll=8)
    lane = lax.broadcasted_iota(jnp.int32, (ext_mo.shape[1], ext_mo.shape[2]), 1)
    low = lane < rank

    def pair(a, b):
        return jnp.where(low, a, b)

    loads[2].wait()
    packed = [pair(ext_mo[FAR + 2 * u], ext_mo[FAR + 2 * u + 1]) for u in range(leaves // 2)]
    own_nm = dot_t(jnp.concatenate(packed, 1), transfer_v[0])
    group_nm[e] = twice(own_nm).astype(BF)

    fine[...] = points[...].astype(F)
    pad = jnp.zeros((13, points.shape[2]), F)

    def own_points(t, carry):
        p = jnp.concatenate([fine[c, pl.ds(t, 1), :] for c in range(3)] + [pad], 0)
        ext_pt[NEAR + t] = p.astype(BF)
        return carry

    lax.fori_loop(0, leaves, own_points, 0, unroll=4)

    def own_tiles(t, carry):
        cols = ext_pt[NEAR + t].astype(F)[:8].T
        for c in range(3):
            tiles[t, c] = jnp.broadcast_to(cols[:, c : c + 1], tiles.shape[2:]).astype(BF)
        return carry

    def sources(s, carry):
        p = ext_pt[s].astype(F)
        for c in range(3):
            rows[s, c] = jnp.broadcast_to(p[c : c + 1], p.shape).astype(BF)
        src_ch[s] = ext_ch[s]
        return carry

    def no_source(s, carry):
        src_ch[s] = jnp.zeros_like(src_ch[s])
        rows[s] = jnp.zeros_like(rows[s])
        return carry

    scale = F(1.0 / (NEAR * points.shape[2] ** 0.5))
    inverse = BF(1.0 / NEAR**2)
    soft = BF(0.25 / NEAR**2)
    copies = tiles.shape[2] // rows.shape[2]

    def tall(row):
        return jnp.concatenate([row] * copies, 0)

    def near(t, carry):
        acc = jnp.zeros(near_acc.shape[1:], F)
        count = near_count[t]
        for j0 in range(0, slots, 2):
            ks = []
            cs = []
            for j in (j0, j0 + 1):
                s = lax.rem(near_list[j, t] - first + NEAR + total, total)
                s = jnp.clip(s, 0, rows.shape[0] - 1)
                gap = (t + NEAR - s).astype(F).astype(BF)
                dx = tiles[t, 0] - tall(rows[s, 0] - gap)
                dy = tiles[t, 1] - tall(rows[s, 1])
                dz = tiles[t, 2] - tall(rows[s, 2])
                square = dx * dx * inverse + soft + (dy * dy + dz * dz)
                ks.append(lax.rsqrt(square))
                live = jnp.where(j < count, F(1), F(0)).astype(BF)
                cs.append(src_ch[s] * live)
            acc = acc + dot_t(jnp.concatenate(cs, 1), jnp.concatenate(ks, 1))
        near_acc[t] = acc * scale
        return carry

    def near_four(u, carry):
        for i in range(4):
            near(4 * u + i, carry)
        return carry

    ahead = lax.rem(g, groups // 2) < groups // EARLY
    lax.fori_loop(0, leaves, own_tiles, 0, unroll=2)

    def own_sources():
        lax.fori_loop(0, NEAR, no_source, 0, unroll=4)
        lax.fori_loop(NEAR + leaves, leaves + 2 * NEAR, no_source, 0, unroll=4)
        lax.fori_loop(NEAR, NEAR + leaves, sources, 0, unroll=4)

    def nm_copy(i):
        peer = lax.rem(e + i, members)
        return pltpu.make_async_remote_copy(
            src_ref=group_nm.at[e],
            dst_ref=group_nm.at[e],
            send_sem=nm_send.at[peer],
            recv_sem=nm_recv.at[e],
            device_id=(g, peer),
            device_id_type=MESH,
        )

    to_right = []
    to_left = []
    for i, (buf, width) in enumerate([(ext_ch, NEAR), (ext_pt, NEAR), (ext_mo, FAR)]):
        to_right.append(
            pltpu.make_async_remote_copy(
                src_ref=buf.at[pl.ds(leaves, width)],
                dst_ref=buf.at[pl.ds(0, width)],
                send_sem=halo_send.at[2 * i],
                recv_sem=halo_recv.at[2 * i],
                device_id=right,
                device_id_type=MESH,
            )
        )
        to_left.append(
            pltpu.make_async_remote_copy(
                src_ref=buf.at[pl.ds(width, width)],
                dst_ref=buf.at[pl.ds(leaves + width, width)],
                send_sem=halo_send.at[2 * i + 1],
                recv_sem=halo_recv.at[2 * i + 1],
                device_id=left,
                device_id_type=MESH,
            )
        )
    def tm_copy(i):
        return pltpu.make_async_remote_copy(
            src_ref=top_own,
            dst_ref=top_all.at[g // kinds],
            send_sem=tm_send.at[i],
            recv_sem=tm_recv.at[g // kinds],
            device_id=(e * share + i, target_member),
            device_id_type=MESH,
        )

    def part_copy(i):
        return pltpu.make_async_remote_copy(
            src_ref=top_part.at[kind],
            dst_ref=top_part.at[kind],
            send_sem=tl_send.at[i],
            recv_sem=tl_recv.at[kind],
            device_id=(g, lax.rem(e + i, members)),
            device_id_type=MESH,
        )

    def enter():
        begin = e * share
        mine = jnp.logical_and(g >= begin, g < begin + share)
        targets = jnp.where(mine, share - 1, share)
        pl.semaphore_wait(barrier, 2 + (members - 1) + targets)

        def nm_start(i, carry):
            nm_copy(i).start()
            return carry

        lax.fori_loop(1, members, nm_start, 0)

        for i in range(3):
            to_right[i].start()
            to_left[i].start()

    def lift_group():
        loads[3].wait()

        def nm_done(i, carry):
            peer = lax.rem(e + i, members)
            pltpu.make_async_remote_copy(
                src_ref=group_nm.at[peer],
                dst_ref=group_nm.at[peer],
                send_sem=nm_send.at[peer],
                recv_sem=nm_recv.at[peer],
                device_id=(g, peer),
                device_id_type=MESH,
            ).wait()
            return carry

        lax.fori_loop(1, members, nm_done, 0)
        top = jnp.zeros((group_nm.shape[1], rank), F)
        for i in range(members):
            top = top + dot_t(group_nm[i][:, :rank], lift_v[0, i])
        top_own[...] = twice(top).astype(BF)

        @pl.when(jnp.logical_and(is_catcher, kind == own_kind))
        def _():
            top_all[g // kinds] = top_own[...]


        for i in range(share):

            @pl.when(e * share + i != g)
            def _(i=i):
                tm_copy(i).start()

    def from_right():
        for i in range(2):
            to_left[i].wait_recv()
        lax.fori_loop(NEAR + leaves, leaves + 2 * NEAR, sources, 0, unroll=4)

    def hand_on():
        loads[4].wait()
        to_left[2].wait_recv()
        to_right[2].wait_recv()

        def couple(t, carry):
            m = []
            for j in range(far_list.shape[0]):
                s = lax.rem(far_list[j, t] - first + FAR + total, total)
                m.append(ext_mo[jnp.clip(s, 0, ext_mo.shape[0] - 1)])
            lhs = [pair(m[j], m[j + 1]) for j in range(0, len(m), 2)]
            coupled[t] = dot_t(jnp.concatenate(lhs, 1), coupling_v[t])
            return carry

        lax.fori_loop(0, leaves, couple, 0, unroll=8)
        loads[5].wait()
        nodes = pair(group_nm[node_list[0, 0]], group_nm[node_list[0, 1]])
        group_loc[...] = dot_t(nodes, ncoup_v[0])

        loads[6].wait()

        @pl.when(is_catcher)
        def _():
            def tm_done(i, carry):
                peer = i * kinds + kind

                @pl.when(peer != g)
                def _():
                    pltpu.make_async_remote_copy(
                        src_ref=top_all.at[i],
                        dst_ref=top_all.at[i],
                        send_sem=tm_send.at[0],
                        recv_sem=tm_recv.at[i],
                        device_id=(peer, g // share),
                        device_id_type=MESH,
                    ).wait_recv()

                return carry

            lax.fori_loop(0, quarter, tm_done, 0)
            terms = []
            for j in range(top_list.shape[1]):
                source = top_list[0, j]
                here = jnp.where(lax.rem(source, kinds) == kind, F(1), F(0)).astype(BF)
                terms.append(top_all[jnp.clip(source // kinds, 0, quarter - 1)] * here)
            lhs = [pair(terms[j], terms[j + 1]) for j in range(0, len(terms), 2)]
            top_part[kind] = twice(dot_t(jnp.concatenate(lhs, 1), tcoup_v[0]))

            def part_start(i, carry):
                part_copy(i).start()
                return carry

            lax.fori_loop(1, members, part_start, 0)

    def from_left():
        for i in range(2):
            to_right[i].wait_recv()
        lax.fori_loop(0, NEAR, sources, 0, unroll=4)

    edge = NEAR // 4
    inner = leaves // 4 - 2 * edge
    half = inner // 2
    late = jnp.logical_not(ahead)

    def choose(a, b):
        return jnp.where(ahead, a, b)

    phases = [
        ([(own_sources, ahead)], edge, choose(inner, 0)),
        ([(enter, True), (own_sources, late), (from_right, ahead)], choose(edge + inner, edge), choose(1, half)),
        (
            [(lift_group, True)],
            choose(edge + inner + 1, edge + half),
            choose(edge - 1, inner - half),
        ),
        ([(from_right, late)], edge + inner, choose(0, edge)),
        ([(from_left, True)], 0, 1),
        ([(hand_on, True)], 1, edge - 1),
    ]

    def phase(p, carry):
        for step in (enter, own_sources, lift_group, from_right, from_left, hand_on):
            now = False
            for i, (steps, _, _) in enumerate(phases):
                for other, takes in steps:
                    if other is step:
                        now = jnp.logical_or(now, jnp.logical_and(p == i, takes))
            pl.when(now)(step)
        begin = 0
        size = 0
        for i, (_, start, count) in enumerate(phases):
            begin = jnp.where(p == i, start, begin)
            size = jnp.where(p == i, count, size)
        lax.fori_loop(begin, begin + size, near_four, 0)
        return carry

    lax.fori_loop(0, len(phases), phase, 0)

    for k in range(kinds):

        @pl.when(catcher + k != e)
        def _(k=k):
            pltpu.make_async_remote_copy(
                src_ref=top_part.at[k],
                dst_ref=top_part.at[k],
                send_sem=tl_send.at[0],
                recv_sem=tl_recv.at[k],
                device_id=(g, catcher + k),
                device_id_type=MESH,
            ).wait_recv()

    top_local = jnp.sum(top_part[...], axis=0)[:, :rank].astype(BF)
    resident = group_loc[...] + jnp.dot(top_local, lift_v[0, e], preferred_element_type=F)
    wide = jnp.dot(resident.astype(BF), transfer_v[0], preferred_element_type=F)
    for u in range(leaves // 2):
        spread[u] = wide[:, 2 * rank * u : 2 * rank * (u + 1)]

    def finish(u, carry):
        base = spread[u]
        for h in range(2):
            t = 2 * u + h
            local = (coupled[t] + base[:, rank * h : rank * (h + 1)]).astype(BF)
            far = jnp.dot(local, basis_v[t], preferred_element_type=F)
            out[t] = (near_acc[t] + far).astype(out.dtype)
        return carry

    lax.fori_loop(0, leaves // 2, finish, 0, unroll=8)

    for h in to_right + to_left:
        h.wait_send()
    for i in range(share):

        @pl.when(e * share + i != g)
        def _(i=i):
            tm_copy(i).wait_send()

    @pl.when(is_catcher)
    def _():
        def part_sent(i, carry):
            part_copy(i).wait_send()
            return carry

        lax.fori_loop(1, members, part_sent, 0)


def shards(
    charges, points, near_list, near_count, basis, far_list, coupling, transfer, node_list,
    node_coupling, lift, top_list, top_coupling,
):
    leaves, right_sides, leaf_pts = charges.shape
    rank = basis.shape[1]
    members = lax.axis_size("grp")
    groups = lax.axis_size("leaf")
    share = groups // members
    kinds = 4
    smem = pl.BlockSpec(memory_space=pltpu.SMEM)
    vmem = pl.BlockSpec(memory_space=pltpu.VMEM)
    hbm = pl.BlockSpec(memory_space=pl.ANY)
    scratch = [
        pltpu.VMEM((leaves + 2 * NEAR, right_sides, leaf_pts), BF),
        pltpu.VMEM((leaves + 2 * NEAR, 16, leaf_pts), BF),
        pltpu.VMEM((leaves + 2 * FAR, right_sides, 2 * rank), BF),
        pltpu.VMEM((3, leaves, leaf_pts), F),
        pltpu.VMEM((leaves + 2 * NEAR, right_sides, leaf_pts), BF),
        pltpu.VMEM((leaves + 2 * NEAR, 3, 16, leaf_pts), BF),
        pltpu.VMEM((leaves, 3, leaf_pts, leaf_pts), BF),
        pltpu.VMEM((leaves, right_sides, leaf_pts), F),
        pltpu.VMEM((leaves // 2, right_sides, 2 * rank), F),
        pltpu.VMEM((leaves, right_sides, rank), F),
        pltpu.VMEM((right_sides, rank), F),
        pltpu.VMEM(basis.shape, BF),
        pltpu.VMEM(coupling.shape, BF),
        pltpu.VMEM(transfer.shape, BF),
        pltpu.VMEM(node_coupling.shape, BF),
        pltpu.VMEM(lift.shape, BF),
        pltpu.VMEM(top_coupling.shape, BF),
        pltpu.VMEM((members, right_sides, 2 * rank), BF),
        pltpu.VMEM((right_sides, 2 * rank), BF),
        pltpu.VMEM((groups // kinds, right_sides, 2 * rank), BF),
        pltpu.VMEM((kinds, right_sides, 2 * rank), F),
        pltpu.SemaphoreType.DMA((7,)),
        pltpu.SemaphoreType.DMA((6,)),
        pltpu.SemaphoreType.DMA((6,)),
        pltpu.SemaphoreType.DMA((members,)),
        pltpu.SemaphoreType.DMA((members,)),
        pltpu.SemaphoreType.DMA((share,)),
        pltpu.SemaphoreType.DMA((groups // kinds,)),
        pltpu.SemaphoreType.DMA((members,)),
        pltpu.SemaphoreType.DMA((kinds,)),
    ]
    result = pl.pallas_call(
        functools.partial(kernel, leaves * members * groups),
        out_shape=jax.ShapeDtypeStruct((leaves, right_sides, leaf_pts), BF),
        in_specs=[smem] * 5 + [hbm, vmem] + [hbm] * 6,
        out_specs=vmem,
        scratch_shapes=scratch,
        compiler_params=pltpu.CompilerParams(
            collective_id=0, has_side_effects=True, vmem_limit_bytes=56 * 2**20
        ),
    )(
        near_list.T, near_count, far_list.T, node_list, top_list, charges, points.transpose(1, 0, 2), basis, coupling,
        transfer, node_coupling, lift, top_coupling,
    )
    return result


def solution(mesh):
    both = ("leaf", "grp")
    return jax.shard_map(
        shards,
        mesh=mesh,
        in_specs=(
            P(both, None, None),
            P(both, None, None),
            P(both, None),
            P(both),
            P(both, None, None),
            P(both, None),
            P(both, None, None),
            P(both, None, None),
            P(both, None),
            P(both, None, None),
            P("leaf", None, None, None),
            P("leaf", None),
            P("leaf", None, None),
        ),
        out_specs=P(both, None, None),
        check_vma=False,
    )
```
